32 devices in a mesh: cp: 16 (over z, x, core), sp: 2 (over y).
Axes of the slice: x: 2, y: 2, z: 4, core: 2. Of those that a mesh axis runs over, the one named last changes fastest.
Arguments:
- queries: bfloat16 [4096, 2048], P('cp', 'sp'), may hold values from -22 to 22
- keys: bfloat16 [4096, 128], P(('cp', 'sp')), may hold values from -5 to 5
- values: bfloat16 [4096, 128], P(('cp', 'sp')), may hold values from -6 to 6
- doc_ids: int32 [32], replicated, may hold values from 0 to 7, never falling along the last dimension, each value on 1 to 8 neighbouring positions
- span_order: int32 [16], replicated, may hold values from 0 to 15, each once
Outputs:
- attended: bfloat16 [4096, 2048], P('cp', 'sp')
The draws below stay inside these ranges and needn't reach their ends.
Inputs may be any that keep to these rules, and one draw needn't show every extreme that they name: doc_ids never falls; each document covers 1 to 8 consecutive blocks, and one covers exactly 8. Index i of cp holds span span_order[i] of the sequence; each span once.
All inputs are finite; a program needn't handle non-finite values.
Results may differ from the reference program's by a relative error of at most 0.0036.
Values may be sent and summed in bfloat16 or wider, within the bound.
No kernel may reach another device: no remote copies, remote signals or barrier semaphores. Data moves between devices by JAX's collectives and lax.ppermute only.
A program may use at most 64 MiB of HBM per device.

```python
import math
import jax
import jax.numpy as jnp
import numpy as np
from jax import lax

HD = 128
HEADS = 16
SPAN = 256
BLK = 128
SEQ = 4096
NBLK = 32
MOST = 8
N_CP = 16


def paired_draw(key):
    key_rows = jnp.clip(jax.random.normal(jax.random.fold_in(key, 11), (SEQ, HD), jnp.float32), -5.0, 5.0)
    query_rows = jnp.clip(jax.random.normal(jax.random.fold_in(key, 14), (SEQ, HEADS, HD), jnp.float32), -5.0, 5.0)
    return (query_rows.reshape(SEQ, HEADS * HD), key_rows)


def draw_queries(key, part):
    query_rows, key_rows = paired_draw(key)
    return query_rows.astype(jnp.bfloat16)


def draw_keys(key, part):
    query_rows, key_rows = paired_draw(key)
    return key_rows.astype(jnp.bfloat16)


def level_of(rng, dims, shards, smallest, top_value):
    loudness = 1.0
    for axis_at, blocks in shards:
        steps = jax.random.uniform(jax.random.fold_in(jax.random.fold_in(rng, 6), axis_at), (blocks,), jnp.float32, smallest / len(shards), top_value / len(shards))
        loudness = loudness * jnp.repeat(jnp.exp(steps), dims[axis_at] // blocks).reshape((-1,) + (1,) * (len(dims) - 1 - axis_at))
    return loudness


def profile(number_of, total, most, skew):
    portions = [(1 << 20) // math.isqrt(standing ** skew) + 1 for standing in range(2, number_of + 1)]
    surplus, holding = total - most - (number_of - 1), [1] * (number_of - 1)
    while surplus > 0:
        movable = [i for i in range(number_of - 1) if holding[i] < most]
        pool, remaining = sum([portions[i] for i in movable]), surplus
        for i in movable:
            addition = min(most - holding[i], max(1, remaining * portions[i] // pool), surplus)
            holding[i] = holding[i] + addition
            surplus = surplus - addition
    return np.array([most] + holding)


def uneven_parts(own_key, amount, total, most, lean):
    if amount == 2:
        one = jax.random.randint(own_key, (), max(1, total - most), min(most, total - 1) + 1)
        return jnp.stack([one, total - one])
    tallies = jnp.asarray(profile(amount, total, most, lean), jnp.int32)
    couples = (amount - 1) // 2
    source_of, receiver = tallies[1:1 + 2 * couples:2], tallies[2:2 + 2 * couples:2]
    margin = jnp.minimum(source_of - 1, most - receiver)
    moved = jax.random.randint(jax.random.fold_in(own_key, 1), (couples,), 0, 1 << 20) % (margin + 1)
    tallies = tallies.at[1:1 + 2 * couples:2].set(source_of - moved).at[2:2 + 2 * couples:2].set(receiver + moved)
    return tallies[jax.random.permutation(jax.random.fold_in(own_key, 2), amount)]


def bell_draw(rng, shape, spread, most, cuts=(), kind=jnp.bfloat16):
    gain = level_of(rng, shape, cuts, -0.22, 0.18) if cuts else 1.0
    values = jax.random.normal(rng, shape, jnp.float32) * spread * gain
    return jnp.minimum(jnp.maximum(values, -most), most).astype(kind)


def setup_inputs(seed: int = 0) -> dict:
    streams_of = jax.random.split(jax.random.key(seed), 6)
    return {
        "queries": draw_queries(jax.random.fold_in(streams_of[5], 71), 0),
        "keys": draw_keys(jax.random.fold_in(streams_of[5], 71), 0),
        "values": bell_draw(streams_of[2], (SEQ, HD), 1.0, 6.0, ((0, 32),)),
        "doc_ids": jnp.searchsorted(jnp.cumsum(uneven_parts(streams_of[3], NBLK // 4, NBLK, MOST, 2)), jnp.arange(NBLK), side="right").astype(jnp.int32),
        "span_order": jax.random.permutation(streams_of[4], N_CP).astype(jnp.int32),
    }


NEGATIVE = -1e+30

def reference(queries, keys, values, doc_ids, span_order):
    score_scale = 1.0 / math.sqrt(HD)

    def to_true(array):
        span_parts = array.reshape((N_CP, SPAN) + array.shape[1:])
        placed = jnp.zeros_like(span_parts).at[span_order].set(span_parts)
        return placed.reshape(array.shape)
    query_true = to_true(queries).reshape(SEQ, HEADS, HD)
    key_true = to_true(keys)
    value_true = to_true(values)
    front_pad = (MOST - 1) * BLK
    window = MOST * BLK
    key_padded = jnp.concatenate([jnp.zeros((front_pad, HD), keys.dtype), key_true], axis=0)
    value_padded = jnp.concatenate([jnp.zeros((front_pad, HD), values.dtype), value_true], axis=0)
    token_doc = jnp.repeat(doc_ids.astype(jnp.int32), BLK)
    doc_padded = jnp.concatenate([jnp.full((front_pad,), -1, jnp.int32), token_doc])

    def attend_block(block_index):
        first = (block_index * BLK).astype(jnp.int32)
        block_query = lax.dynamic_slice_in_dim(query_true, first, BLK, 0).astype(jnp.float32)
        block_key = lax.dynamic_slice_in_dim(key_padded, first, window, 0).astype(jnp.float32)
        block_value = lax.dynamic_slice_in_dim(value_padded, first, window, 0).astype(jnp.float32)
        query_doc = lax.dynamic_slice_in_dim(token_doc, first, BLK, 0)
        key_doc = lax.dynamic_slice_in_dim(doc_padded, first, window, 0)
        query_pos = first + jnp.arange(BLK, dtype=jnp.int32)
        key_pos = first - front_pad + jnp.arange(window, dtype=jnp.int32)
        allowed = (key_pos[None, :] <= query_pos[:, None]) & (key_doc[None, :] == query_doc[:, None])
        scores = jnp.einsum('qhd,kd->hqk', block_query, block_key, precision=lax.Precision.HIGHEST) * score_scale
        masked = jnp.where(allowed[None], scores, NEGATIVE)
        row_max = lax.optimization_barrier(jnp.max(masked, axis=2, keepdims=True))
        raw = jnp.where(allowed[None], jnp.exp(masked - row_max), 0.0)
        row_total = lax.optimization_barrier(jnp.sum(raw, axis=2))
        weights = lax.optimization_barrier(raw.astype(jnp.bfloat16)).astype(jnp.float32)
        numer = jnp.einsum('hqk,kd->qhd', weights, block_value, precision=lax.Precision.HIGHEST)
        return (numer / jnp.transpose(row_total)[:, :, None]).astype(jnp.bfloat16)
    blocks = lax.map(attend_block, jnp.arange(NBLK, dtype=jnp.int32))
    result_true = blocks.reshape(N_CP, SPAN, HEADS * HD)
    return result_true[span_order].reshape(SEQ, HEADS * HD)
```

```python
import functools
import math

import jax
import jax.numpy as jnp
from jax import lax
from jax.experimental import pallas as pl
from jax.experimental.pallas import tpu as pltpu
from jax.sharding import PartitionSpec as P

HD = 128
SPAN = 256
BLK = 128
NEGATIVE = -1e30
SCALE2 = math.log2(math.e) / math.sqrt(HD)


def flip(array, axis, size, mask):
    return lax.ppermute(array, axis, [(i, i ^ mask) for i in range(size)])


def select_kernel(reach, order_ref, cp_ref, *refs):
    sources, out_ref = refs[:-1], refs[-1]
    cp = cp_ref[0]
    own_span = order_ref[cp]
    count = order_ref.shape[0]
    for back in range(1, reach + 1):
        span = jnp.maximum(own_span - back, 0)
        holder = jnp.int32(0)
        for index in range(count):
            holder = jnp.where(order_ref[index] == span, jnp.int32(index), holder)
        apart = holder ^ cp
        slot = apart >> 2
        for low, source in enumerate(sources):

            @pl.when((apart & 3) == low)
            def _():
                out_ref[back - 1] = source[slot]


def attend_half(half, span, doc_ref, q_ref, own_ref, prev_ref, buf, scores, max_ref, acc_ref, fresh):
    reach = prev_ref.shape[0]
    heads = q_ref.shape[1] // HD
    pairs = scores.shape[0]
    buf[0:BLK, 0 : 2 * HD] = own_ref[...]
    for back in range(reach):
        buf[(back + 1) * BLK : (back + 2) * BLK, 0 : 2 * HD] = prev_ref[back]
    rows = lax.broadcasted_iota(jnp.int32, (BLK, 2 * BLK), 0)
    cols = lax.broadcasted_iota(jnp.int32, (BLK, 2 * BLK), 1)
    for a in range(2):
        doc = doc_ref[2 * span + a]
        first = jnp.where(half <= a, 0, 1)
        count = jnp.int32(0)
        for back in range(reach + 1):
            block = 2 * (span - back) + half
            same = doc_ref[jnp.maximum(block, 0)] == doc
            inside = (block >= 0) & (back >= first)
            count = count + jnp.where(same & inside, 1, 0)
        diagonal = half == a

        if fresh:
            max_ref[a] = jnp.full(max_ref.shape[1:], NEGATIVE, jnp.float32)
            acc_ref[a] = jnp.zeros(acc_ref.shape[1:], jnp.float32)

        @pl.when(count > 0)
        def _():
            old_max = max_ref[a]

            def score_step(pair, unused):
                start = pl.multiple_of((first + 2 * pair) * BLK, BLK)
                key_pair = buf[pl.ds(start, 2 * BLK), 0:HD]
                limit = jnp.where(diagonal & (pair == 0), 0, 2 * BLK)
                open_low = (cols < BLK) & (cols <= rows + limit)
                open_high = (cols >= BLK) & (cols < (count - 2 * pair) * BLK)
                bias = jnp.where(open_low | open_high, 0.0, NEGATIVE)
                for h in range(heads):
                    block = lax.dot_general(
                        q_ref[a * BLK : (a + 1) * BLK, h * HD : (h + 1) * HD],
                        key_pair,
                        (((1,), (1,)), ((), ())),
                        preferred_element_type=jnp.float32,
                    )
                    block = block + bias
                    scores[pair, h] = block
                    best = jnp.maximum(block[:, :BLK], block[:, BLK:])
                    max_ref[a, h] = jnp.maximum(max_ref[a, h], best)
                return unused

            steps = (count + 1) // 2
            lax.fori_loop(0, steps, score_step, 0)
            for h in range(heads):
                top = jnp.max(max_ref[a, h], axis=1, keepdims=True)
                top = jnp.broadcast_to(top, (BLK, HD))
                max_ref[a, h] = top
                if not fresh:
                    keep = jnp.exp2((old_max[h] - top) * SCALE2)
                    acc_ref[a, h, :, 0:HD] = acc_ref[a, h, :, 0:HD] * keep
                    acc_ref[a, h, :, HD:] = acc_ref[a, h, :, HD:] * keep

            def value_step(pair, unused):
                start = pl.multiple_of((first + 2 * pair) * BLK, BLK)
                value_pair = buf[pl.ds(start, 2 * BLK), HD : 3 * HD]
                for h in range(heads):
                    top = max_ref[a, h]
                    low = jnp.exp2((scores[pair, h, :, :BLK] - top) * SCALE2)
                    high = jnp.exp2((scores[pair, h, :, BLK:] - top) * SCALE2)
                    weights = jnp.concatenate([low, high], axis=1).astype(jnp.bfloat16)
                    acc_ref[a, h] += jnp.dot(weights, value_pair, preferred_element_type=jnp.float32)
                return unused

            lax.fori_loop(0, steps, value_step, 0)


def attend_kernel(
    doc_ref, order_ref, place_ref, q_ref, own_ref, prev_ref, other_own_ref, other_prev_ref, out_ref,
    buf, scores, max_ref, acc_ref,
):
    span = order_ref[place_ref[0]]
    half = place_ref[1]
    heads = q_ref.shape[1] // HD
    buf[:, 2 * HD :] = jnp.ones((buf.shape[0], HD), buf.dtype)
    attend_half(half, span, doc_ref, q_ref, own_ref, prev_ref, buf, scores, max_ref, acc_ref, True)
    attend_half(1 - half, span, doc_ref, q_ref, other_own_ref, other_prev_ref, buf, scores, max_ref, acc_ref, False)
    for a in range(2):
        for h in range(heads):
            result = acc_ref[a, h, :, 0:HD] / acc_ref[a, h, :, HD:]
            out_ref[a * BLK : (a + 1) * BLK, h * HD : (h + 1) * HD] = result.astype(out_ref.dtype)


VMEM = pl.BlockSpec(memory_space=pltpu.VMEM)
SMEM = pl.BlockSpec(memory_space=pltpu.SMEM)


def select(order, place, sources, reach):
    return pl.pallas_call(
        functools.partial(select_kernel, reach),
        out_shape=jax.ShapeDtypeStruct((reach,) + sources[0].shape[1:], sources[0].dtype),
        in_specs=[SMEM, SMEM] + [VMEM] * len(sources),
        out_specs=VMEM,
        name="select",
    )(order, place, *sources)


def attend(docs, order, place, queries, own, prev, other_own, other_prev):
    reach = prev.shape[0]
    heads = queries.shape[1] // HD
    pairs = (reach + 1) // 2
    slots = 2 * pairs + 1
    return pl.pallas_call(
        attend_kernel,
        out_shape=jax.ShapeDtypeStruct(queries.shape, queries.dtype),
        in_specs=[SMEM] * 3 + [VMEM] * 5,
        out_specs=VMEM,
        scratch_shapes=[
            pltpu.VMEM((slots * BLK, 3 * HD), jnp.bfloat16),
            pltpu.VMEM((pairs, heads, BLK, 2 * BLK), jnp.float32),
            pltpu.VMEM((2, heads, BLK, HD), jnp.float32),
            pltpu.VMEM((2, heads, BLK, 2 * HD), jnp.float32),
        ],
        compiler_params=pltpu.CompilerParams(vmem_limit_bytes=32 * 1024 * 1024),
        name="attend",
    )(docs, order, place, queries, own, prev, other_own, other_prev)


def shards(cp_size, sp_size, queries, keys, values, doc_ids, span_order):
    longest = doc_ids.shape[0] // 4
    reach = longest // 2
    cp_index = lax.axis_index("cp").astype(jnp.int32)
    own = jnp.concatenate([keys, values], axis=1)
    if cp_size == 16 and sp_size == 2:
        place = jnp.stack([cp_index, lax.axis_index("sp").astype(jnp.int32)])
        near = [flip(own, "cp", cp_size, 4 * j) for j in (3, 2, 1)][::-1]
        line = jnp.stack([own] + near)
        side = flip(line, "cp", cp_size, 2)
        other_own = flip(own, "sp", sp_size, 1)
        core_line = flip(line, "cp", cp_size, 1)
        core_side = flip(side, "cp", cp_size, 1)
        prev = select(span_order, place, [line, core_line, side, core_side], reach)
        other_prev = flip(prev, "sp", sp_size, 1)
    else:
        place = jnp.stack([cp_index, jnp.int32(0)])
        pair = lax.all_gather(own, ("cp", "sp"), axis=0, tiled=True).reshape(cp_size, 2, BLK, 2 * HD)
        holder = jnp.argsort(span_order)
        back = jnp.maximum(span_order[cp_index] - jnp.arange(reach + 1, dtype=jnp.int32), 0)
        chosen = pair[holder[back]]
        own, other_own = chosen[0, 0], chosen[0, 1]
        prev, other_prev = chosen[1:, 0], chosen[1:, 1]
    return attend(doc_ids, span_order, place, queries, own, prev, other_own, other_prev)


def solution(mesh):
    in_specs = (P("cp", "sp"), P(("cp", "sp"), None), P(("cp", "sp"), None), P(), P())
    out_specs = P("cp", "sp")
    body = functools.partial(shards, mesh.shape["cp"], mesh.shape["sp"])
    return jax.shard_map(body, mesh=mesh, in_specs=in_specs, out_specs=out_specs, check_vma=False)
```

```python
import functools
import math

import jax
import jax.numpy as jnp
from jax import lax
from jax.experimental import pallas as pl
from jax.experimental.pallas import tpu as pltpu
from jax.sharding import PartitionSpec as P

HD = 128
SPAN = 256
BLK = 128
NEGATIVE = -1e30
SCALE2 = math.log2(math.e) / math.sqrt(HD)


def flip(array, axis, size, mask):
    return lax.ppermute(array, axis, [(i, i ^ mask) for i in range(size)])


def select_kernel(reach, order_ref, cp_ref, *refs):
    sources, out_ref = refs[:-1], refs[-1]
    cp = cp_ref[0]
    own_span = order_ref[cp]
    count = order_ref.shape[0]
    for back in range(1, reach + 1):
        span = jnp.maximum(own_span - back, 0)
        holder = jnp.int32(0)
        for index in range(count):
            holder = jnp.where(order_ref[index] == span, jnp.int32(index), holder)
        apart = holder ^ cp
        slot = apart >> 2
        for low, source in enumerate(sources):

            @pl.when((apart & 3) == low)
            def _():
                out_ref[back - 1] = source[slot]


def fold_half(half, span, doc_ref, q_ref, own_ref, prev_ref, start_max, buf, scores, max_ref, acc_ref):
    reach = prev_ref.shape[0]
    heads = q_ref.shape[1] // HD
    buf[0:BLK, 0 : 2 * HD] = own_ref[...]
    for back in range(reach):
        buf[(back + 1) * BLK : (back + 2) * BLK, 0 : 2 * HD] = prev_ref[back]
    buf[:, 2 * HD :] = jnp.ones((buf.shape[0], HD), buf.dtype)
    rows = lax.broadcasted_iota(jnp.int32, (BLK, 2 * BLK), 0)
    cols = lax.broadcasted_iota(jnp.int32, (BLK, 2 * BLK), 1)
    for a in range(2):
        doc = doc_ref[2 * span + a]
        first = jnp.where(half <= a, 0, 1)
        count = jnp.int32(0)
        for back in range(reach + 1):
            block = 2 * (span - back) + half
            same = doc_ref[jnp.maximum(block, 0)] == doc
            inside = (block >= 0) & (back >= first)
            count = count + jnp.where(same & inside, 1, 0)
        diagonal = half == a
        steps = (count + 1) // 2
        if start_max is None:
            max_ref[a] = jnp.full(max_ref.shape[1:], NEGATIVE, jnp.float32)
        else:
            max_ref[a] = start_max[a]
        acc_ref[a] = jnp.zeros(acc_ref.shape[1:], jnp.float32)

        @pl.when(count > 0)
        def _():
            def score_step(pair, unused):
                start = pl.multiple_of((first + 2 * pair) * BLK, BLK)
                key_pair = buf[pl.ds(start, 2 * BLK), 0:HD]
                limit = jnp.where(diagonal & (pair == 0), 0, 2 * BLK)
                open_low = (cols < BLK) & (cols <= rows + limit)
                open_high = (cols >= BLK) & (cols < (count - 2 * pair) * BLK)
                bias = jnp.where(open_low | open_high, 0.0, NEGATIVE)
                for h in range(heads):
                    block = lax.dot_general(
                        q_ref[a * BLK : (a + 1) * BLK, h * HD : (h + 1) * HD],
                        key_pair,
                        (((1,), (1,)), ((), ())),
                        preferred_element_type=jnp.float32,
                    )
                    block = block + bias
                    scores[pair, h] = block
                    best = jnp.maximum(block[:, :BLK], block[:, BLK:])
                    max_ref[a, h] = jnp.maximum(max_ref[a, h], best)
                return unused

            lax.fori_loop(0, steps, score_step, 0)
            for h in range(heads):
                top = jnp.max(max_ref[a, h], axis=1, keepdims=True)
                max_ref[a, h] = jnp.broadcast_to(top, (BLK, HD))

            def value_step(pair, unused):
                start = pl.multiple_of((first + 2 * pair) * BLK, BLK)
                value_pair = buf[pl.ds(start, 2 * BLK), HD : 3 * HD]
                for h in range(heads):
                    top = max_ref[a, h]
                    low = jnp.exp2((scores[pair, h, :, :BLK] - top) * SCALE2)
                    high = jnp.exp2((scores[pair, h, :, BLK:] - top) * SCALE2)
                    weights = jnp.concatenate([low, high], axis=1).astype(jnp.bfloat16)
                    acc_ref[a, h] += jnp.dot(weights, value_pair, preferred_element_type=jnp.float32)
                return unused

            lax.fori_loop(0, steps, value_step, 0)


def first_kernel(doc_ref, order_ref, place_ref, q_ref, own_ref, prev_ref, max_ref, acc_ref, buf, scores):
    span, half = order_ref[place_ref[0]], place_ref[1]
    fold_half(half, span, doc_ref, q_ref, own_ref, prev_ref, None, buf, scores, max_ref, acc_ref)


def second_kernel(
    doc_ref, order_ref, place_ref, q_ref, own_ref, prev_ref, old_max, old_acc, out_ref, buf, scores, max_ref, acc_ref
):
    span, half = order_ref[place_ref[0]], 1 - place_ref[1]
    fold_half(half, span, doc_ref, q_ref, own_ref, prev_ref, old_max, buf, scores, max_ref, acc_ref)
    for a in range(2):
        for h in range(q_ref.shape[1] // HD):
            keep = jnp.exp2((old_max[a, h] - max_ref[a, h]) * SCALE2)
            total = old_acc[a, h, :, HD:] * keep + acc_ref[a, h, :, HD:]
            result = (old_acc[a, h, :, 0:HD] * keep + acc_ref[a, h, :, 0:HD]) / total
            out_ref[a * BLK : (a + 1) * BLK, h * HD : (h + 1) * HD] = result.astype(out_ref.dtype)


VMEM = pl.BlockSpec(memory_space=pltpu.VMEM)
SMEM = pl.BlockSpec(memory_space=pltpu.SMEM)


def select(order, place, sources, reach):
    return pl.pallas_call(
        functools.partial(select_kernel, reach),
        out_shape=jax.ShapeDtypeStruct((reach,) + sources[0].shape[1:], sources[0].dtype),
        in_specs=[SMEM, SMEM] + [VMEM] * len(sources),
        out_specs=VMEM,
        compiler_params=pltpu.CompilerParams(vmem_limit_bytes=4 * 1024 * 1024),
        name="select",
    )(order, place, *sources)


def attend(docs, order, place, queries, own, prev, state=None):
    reach = prev.shape[0]
    heads = queries.shape[1] // HD
    pairs = (reach + 1) // 2
    max_shape, acc_shape = (2, heads, BLK, HD), (2, heads, BLK, 2 * HD)
    scratch = [
        pltpu.VMEM(((2 * pairs + 1) * BLK, 3 * HD), jnp.bfloat16),
        pltpu.VMEM((pairs, heads, BLK, 2 * BLK), jnp.float32),
    ]
    shared = dict(
        compiler_params=pltpu.CompilerParams(vmem_limit_bytes=12 * 1024 * 1024),
        cost_estimate=pl.CostEstimate(flops=1 << 30, bytes_accessed=1 << 22, transcendentals=1 << 20),
    )
    if state is None:
        return pl.pallas_call(
            first_kernel,
            out_shape=[jax.ShapeDtypeStruct(max_shape, jnp.float32), jax.ShapeDtypeStruct(acc_shape, jnp.float32)],
            in_specs=[SMEM] * 3 + [VMEM] * 3,
            out_specs=[VMEM, VMEM],
            scratch_shapes=scratch,
            name="attend_first",
            **shared,
        )(docs, order, place, queries, own, prev)
    return pl.pallas_call(
        second_kernel,
        out_shape=jax.ShapeDtypeStruct(queries.shape, queries.dtype),
        in_specs=[SMEM] * 3 + [VMEM] * 5,
        out_specs=VMEM,
        scratch_shapes=scratch + [pltpu.VMEM(max_shape, jnp.float32), pltpu.VMEM(acc_shape, jnp.float32)],
        name="attend_second",
        **shared,
    )(docs, order, place, queries, own, prev, *state)


def shards(cp_size, sp_size, queries, keys, values, doc_ids, span_order):
    longest = doc_ids.shape[0] // 4
    reach = longest // 2
    cp_index = lax.axis_index("cp").astype(jnp.int32)
    own = jnp.concatenate([keys, values], axis=1)
    if cp_size == 16 and sp_size == 2:
        place = jnp.stack([cp_index, lax.axis_index("sp").astype(jnp.int32)])
        near = [flip(own, "cp", cp_size, 4 * j) for j in (3, 2, 1)][::-1]
        line = jnp.stack([own] + near)
        side = flip(line, "cp", cp_size, 2)
        other_own = flip(own, "sp", sp_size, 1)
        core_line = flip(line, "cp", cp_size, 1)
        side, other_own = lax.optimization_barrier((side, other_own))
        core_side = flip(side, "cp", cp_size, 1)
        prev = select(span_order, place, [line, core_line, side, core_side], reach)
        other_prev = flip(prev, "sp", sp_size, 1)
    else:
        place = jnp.stack([cp_index, jnp.int32(0)])
        pair = lax.all_gather(own, ("cp", "sp"), axis=0, tiled=True).reshape(cp_size, 2, BLK, 2 * HD)
        holder = jnp.argsort(span_order)
        back = jnp.maximum(span_order[cp_index] - jnp.arange(reach + 1, dtype=jnp.int32), 0)
        chosen = pair[holder[back]]
        own, other_own = chosen[0, 0], chosen[0, 1]
        prev, other_prev = chosen[1:, 0], chosen[1:, 1]
    state = attend(doc_ids, span_order, place, queries, own, prev)
    return attend(doc_ids, span_order, place, queries, other_own, other_prev, state)


def solution(mesh):
    in_specs = (P("cp", "sp"), P(("cp", "sp"), None), P(("cp", "sp"), None), P(), P())
    out_specs = P("cp", "sp")
    body = functools.partial(shards, mesh.shape["cp"], mesh.shape["sp"])
    return jax.shard_map(body, mesh=mesh, in_specs=in_specs, out_specs=out_specs, check_vma=False)
```

```python
import functools
import math

import jax
import jax.numpy as jnp
from jax import lax
from jax.experimental import pallas as pl
from jax.experimental.pallas import tpu as pltpu
from jax.sharding import PartitionSpec as P

HD = 128
SPAN = 256
BLK = 128
NEGATIVE = -1e30
HEAD = 2
SCALE2 = math.log2(math.e) / math.sqrt(HD)


def flip(array, axis, size, mask):
    return lax.ppermute(array, axis, [(i, i ^ mask) for i in range(size)])


def select_kernel(places, meta_ref, *refs):
    sources, out_ref = refs[:-1], refs[-1]
    cp = meta_ref[0]
    own_span = meta_ref[HEAD + cp]
    for back in range(1, out_ref.shape[0] // BLK + 1):
        span = jnp.maximum(own_span - back, 0)
        holder = jnp.int32(0)
        for index in range(len(places)):
            holder = jnp.where(meta_ref[HEAD + index] == span, jnp.int32(index), holder)
        apart = holder ^ cp
        for distance, (source, slot) in enumerate(places):

            @pl.when(apart == distance)
            def _():
                out_ref[(back - 1) * BLK : back * BLK, :] = sources[source][slot]


def layout(meta_ref, cp_size):
    span = meta_ref[HEAD + meta_ref[0]]
    doc_at = HEAD + cp_size
    return span, doc_at, meta_ref[doc_at + 2 * span] == meta_ref[doc_at + 2 * span + 1]


def earlier_count(meta_ref, span, doc_at, half, reach):
    doc = meta_ref[doc_at + 2 * span]
    count = jnp.int32(0)
    for back in range(1, reach + 1):
        block = 2 * (span - back) + half
        held = (block >= 0) & (meta_ref[doc_at + jnp.maximum(block, 0)] == doc)
        count = count + jnp.where(held, 1, 0)
    return count


def score(q_ref, a, h, keys):
    return lax.dot_general(
        q_ref[a * BLK : (a + 1) * BLK, h * HD : (h + 1) * HD],
        keys,
        (((1,), (1,)), ((), ())),
        preferred_element_type=jnp.float32,
    )


def weigh(scores, top):
    parts = [jnp.exp2((scores[:, c : c + BLK] - top) * SCALE2) for c in range(0, scores.shape[1], BLK)]
    return jnp.concatenate(parts, axis=1).astype(jnp.bfloat16)


def with_ones(values):
    return jnp.concatenate([values, jnp.ones_like(values)], axis=1)


def fold(a, count, q_ref, buf, scores, max_ref, acc_ref, own):
    heads = q_ref.shape[1] // HD
    pairs = count // 2
    odd = count % 2 == 1

    def keep(pair, h, block):
        best = block[:, :BLK]
        if block.shape[1] > BLK:
            best = jnp.maximum(best, block[:, BLK:])
        scores[pair, h, :, : block.shape[1]] = block
        max_ref[a, h] = jnp.maximum(max_ref[a, h], best)

    def score_step(pair, unused):
        keys = buf[pl.ds(pl.multiple_of(pair * 2 * BLK, BLK), 2 * BLK), 0:HD]
        for h in range(heads):
            keep(pair, h, score(q_ref, a, h, keys))
        return unused

    if own is not None:
        own_rows, own_bias = own
        width = own_bias.shape[1]
        last = scores.shape[0] - 1
        for h in range(heads):
            block = score(q_ref, a, h, own_rows[:, 0:HD]) + own_bias
            scores[last, h, :, :width] = block
            max_ref[a, h] = jnp.maximum(block[:, :BLK], block[:, width - BLK :])
    lax.fori_loop(0, pairs, score_step, 0)

    @pl.when(odd)
    def _():
        keys = buf[pl.ds(pl.multiple_of(pairs * 2 * BLK, BLK), BLK), 0:HD]
        for h in range(heads):
            keep(pairs, h, score(q_ref, a, h, keys))

    for h in range(heads):
        top = jnp.max(max_ref[a, h], axis=1, keepdims=True)
        max_ref[a, h] = jnp.broadcast_to(top, (BLK, HD))

    def value_step(pair, unused):
        values = with_ones(buf[pl.ds(pl.multiple_of(pair * 2 * BLK, BLK), 2 * BLK), HD:])
        for h in range(heads):
            weights = weigh(scores[pair, h], max_ref[a, h])
            acc_ref[a, h] += jnp.dot(weights, values, preferred_element_type=jnp.float32)
        return unused

    if own is not None:
        values = with_ones(own_rows[:, HD:])
        for h in range(heads):
            weights = weigh(scores[last, h, :, :width], max_ref[a, h])
            acc_ref[a, h] = jnp.dot(weights, values, preferred_element_type=jnp.float32)
    lax.fori_loop(0, pairs, value_step, 0)

    @pl.when(odd)
    def _():
        values = with_ones(buf[pl.ds(pl.multiple_of(pairs * 2 * BLK, BLK), BLK), HD:])
        for h in range(heads):
            weights = weigh(scores[pairs, h, :, :BLK], max_ref[a, h])
            acc_ref[a, h] += jnp.dot(weights, values, preferred_element_type=jnp.float32)


def first_kernel(cp_size, meta_ref, q_ref, own_ref, other_ref, prev_ref, max_ref, acc_ref, scores):
    half = meta_ref[1]
    span, doc_at, same = layout(meta_ref, cp_size)
    count = earlier_count(meta_ref, span, doc_at, half, prev_ref.shape[0] // BLK)
    swap = half == 1
    mine, other = own_ref[...], other_ref[...]
    low, high = jnp.where(swap, other, mine), jnp.where(swap, mine, other)
    rows = lax.broadcasted_iota(jnp.int32, (BLK, BLK), 0)
    cols = lax.broadcasted_iota(jnp.int32, (BLK, BLK), 1)
    causal = jnp.where(cols <= rows, 0.0, NEGATIVE)
    before = jnp.where(same, jnp.zeros_like(causal), NEGATIVE)
    fold(0, count, q_ref, prev_ref, scores, max_ref, acc_ref, (low, causal))
    both = jnp.concatenate([low, high], axis=0), jnp.concatenate([before, causal], axis=1)
    fold(1, jnp.where(same, count, 0), q_ref, prev_ref, scores, max_ref, acc_ref, both)


def second_kernel(cp_size, meta_ref, q_ref, prev_ref, old_max, old_acc, out_ref, scores, max_ref, acc_ref):
    half = 1 - meta_ref[1]
    span, doc_at, same = layout(meta_ref, cp_size)
    count = earlier_count(meta_ref, span, doc_at, half, prev_ref.shape[0] // BLK)
    for a in range(2):
        used = count if a == 0 else jnp.where(same, count, 0)
        rows = slice(a * BLK, (a + 1) * BLK)

        @pl.when(used == 0)
        def _():
            for h in range(q_ref.shape[1] // HD):
                result = old_acc[a, h, :, 0:HD] / old_acc[a, h, :, HD:]
                out_ref[rows, h * HD : (h + 1) * HD] = result.astype(out_ref.dtype)

        @pl.when(used > 0)
        def _():
            max_ref[a] = old_max[a]
            acc_ref[a] = jnp.zeros(acc_ref.shape[1:], jnp.float32)
            fold(a, used, q_ref, prev_ref, scores, max_ref, acc_ref, None)
            for h in range(q_ref.shape[1] // HD):
                fade = jnp.exp2((old_max[a, h] - max_ref[a, h]) * SCALE2)
                total = old_acc[a, h, :, HD:] * fade + acc_ref[a, h, :, HD:]
                result = (old_acc[a, h, :, 0:HD] * fade + acc_ref[a, h, :, 0:HD]) / total
                out_ref[rows, h * HD : (h + 1) * HD] = result.astype(out_ref.dtype)


VMEM = pl.BlockSpec(memory_space=pltpu.VMEM)
SMEM = pl.BlockSpec(memory_space=pltpu.SMEM)
SHARED = dict(
    compiler_params=pltpu.CompilerParams(vmem_limit_bytes=16 * 1024 * 1024),
    cost_estimate=pl.CostEstimate(flops=1 << 30, bytes_accessed=1 << 22, transcendentals=1 << 20),
)


def select(meta, sources, places, reach):
    return pl.pallas_call(
        functools.partial(select_kernel, places),
        out_shape=jax.ShapeDtypeStruct((reach * BLK, 2 * HD), jnp.bfloat16),
        in_specs=[SMEM] + [VMEM] * len(sources),
        out_specs=VMEM,
        compiler_params=pltpu.CompilerParams(vmem_limit_bytes=4 * 1024 * 1024),
        name="select",
    )(meta, *sources)


def attend_first(cp_size, meta, queries, own, other, prev):
    heads = queries.shape[1] // HD
    pairs = prev.shape[0] // (2 * BLK)
    max_shape, acc_shape = (2, heads, BLK, HD), (2, heads, BLK, 2 * HD)
    return pl.pallas_call(
        functools.partial(first_kernel, cp_size),
        out_shape=[jax.ShapeDtypeStruct(max_shape, jnp.float32), jax.ShapeDtypeStruct(acc_shape, jnp.float32)],
        in_specs=[SMEM] + [VMEM] * 4,
        out_specs=[VMEM, VMEM],
        scratch_shapes=[pltpu.VMEM((pairs + 1, heads, BLK, 2 * BLK), jnp.float32)],
        name="attend_first",
        **SHARED,
    )(meta, queries, own, other, prev)


def attend_second(cp_size, meta, queries, prev, state):
    heads = queries.shape[1] // HD
    pairs = prev.shape[0] // (2 * BLK)
    return pl.pallas_call(
        functools.partial(second_kernel, cp_size),
        out_shape=jax.ShapeDtypeStruct(queries.shape, queries.dtype),
        in_specs=[SMEM] + [VMEM] * 4,
        out_specs=VMEM,
        scratch_shapes=[pltpu.VMEM((pairs, heads, BLK, 2 * BLK), jnp.float32)]
        + [pltpu.VMEM(part.shape, jnp.float32) for part in state],
        name="attend_second",
        **SHARED,
    )(meta, queries, prev, *state)


def shards(cp_size, sp_size, queries, keys, values, doc_ids, span_order):
    reach = doc_ids.shape[0] // 8
    staged = cp_size == 16 and sp_size == 2
    cp_index = lax.axis_index("cp").astype(jnp.int32)
    half = lax.axis_index("sp").astype(jnp.int32) if staged else jnp.int32(0)
    meta = jnp.concatenate([jnp.stack([cp_index, half]), span_order, doc_ids])
    own = lax.pad(keys, jnp.bfloat16(0), ((0, 0, 0), (0, HD, 0)))
    own = own + lax.pad(values, jnp.bfloat16(0), ((0, 0, 0), (HD, 0, 0)))
    if staged:
        by_x = lambda array: flip(array, "cp", cp_size, 2)
        by_y = lambda array: flip(array, "sp", sp_size, 1)
        by_core = lambda array: flip(array, "cp", cp_size, 1)
        far = {j: flip(own, "cp", cp_size, 4 * j) for j in (3, 2, 1)}
        far[0] = own
        other = by_y(own)
        sources, places = [], {}
        for group in ((3, 0), (1, 2)):
            line = jnp.stack([far[j] for j in group])
            side, meta, other = lax.optimization_barrier((by_x(line), meta, other))
            for flips, array in ((0, line), (2, side), (1, by_core(line)), (3, by_core(side))):
                for slot, j in enumerate(group):
                    places[4 * j ^ flips] = (len(sources), slot)
                sources.append(array)
        prev = select(meta, sources, [places[distance] for distance in range(cp_size)], reach)
        other_prev = by_y(prev)
    else:
        pair = lax.all_gather(own, ("cp", "sp"), axis=0, tiled=True).reshape(cp_size, 2, BLK, 2 * HD)
        holder = jnp.argsort(span_order)
        back = jnp.maximum(span_order[cp_index] - jnp.arange(reach + 1, dtype=jnp.int32), 0)
        chosen = pair[holder[back]]
        own, other = chosen[0, 0], chosen[0, 1]
        prev, other_prev = (chosen[1:, k].reshape(reach * BLK, 2 * HD) for k in (0, 1))
    state = attend_first(cp_size, meta, queries, own, other, prev)
    return attend_second(cp_size, meta, queries, other_prev, state)


def solution(mesh):
    in_specs = (P("cp", "sp"), P(("cp", "sp"), None), P(("cp", "sp"), None), P(), P())
    out_specs = P("cp", "sp")
    body = functools.partial(shards, mesh.shape["cp"], mesh.shape["sp"])
    return jax.shard_map(body, mesh=mesh, in_specs=in_specs, out_specs=out_specs, check_vma=False)
```

```python
import functools
import math

import jax
import jax.numpy as jnp
from jax import lax
from jax.experimental import pallas as pl
from jax.experimental.pallas import tpu as pltpu
from jax.sharding import PartitionSpec as P

HD = 128
SPAN = 256
BLK = 128
NEGATIVE = -1e30
HEAD = 2
SCALE2 = math.log2(math.e) / math.sqrt(HD)
LINES = ((3, 0), (1, 2))


def flip(array, axis, size, mask):
    return lax.ppermute(array, axis, [(i, i ^ mask) for i in range(size)])


def locate(apart):
    line = apart >> 2
    group = (line ^ (line >> 1)) & 1
    return group * 4 + (apart & 1) * 2 + ((apart >> 1) & 1), 1 - (line & 1)


def select_kernel(cp_size, meta_ref, *refs):
    sources, (keys_ref, values_ref) = refs[:-2], refs[-2:]
    cp = meta_ref[0]
    own_span = meta_ref[HEAD + cp]
    for back in range(1, keys_ref.shape[0] // BLK + 1):
        span = jnp.maximum(own_span - back, 0)
        holder = jnp.int32(0)
        for index in range(cp_size):
            holder = jnp.where(meta_ref[HEAD + index] == span, jnp.int32(index), holder)
        source, slot = locate(holder ^ cp)
        for index, ref in enumerate(sources):

            @pl.when(source == index)
            def _():
                rows = slice((back - 1) * BLK, back * BLK)
                keys_ref[rows, :] = ref[slot, :, 0:HD]
                values_ref[rows, :] = ref[slot, :, HD:]


def extent(meta_ref, cp_size, half, reach):
    span = meta_ref[HEAD + meta_ref[0]]
    doc_at = HEAD + cp_size
    doc = meta_ref[doc_at + 2 * span]
    count = jnp.int32(0)
    for back in range(1, reach + 1):
        block = 2 * (span - back) + half
        held = (block >= 0) & (meta_ref[doc_at + jnp.maximum(block, 0)] == doc)
        count = count + jnp.where(held, 1, 0)
    return count, doc == meta_ref[doc_at + 2 * span + 1]


def stack_kernel(q_ref, out_ref, sems):
    heads = out_ref.shape[1] // BLK
    copies = [
        pltpu.make_async_copy(
            q_ref.at[pl.ds(a * BLK, BLK), pl.ds(h * HD, HD)], out_ref.at[a, pl.ds(h * BLK, BLK), :], sems.at[a, h]
        )
        for a in range(2)
        for h in range(heads)
    ]
    for copy in copies:
        copy.start()
    for copy in copies:
        copy.wait()


def score(queries, keys):
    return lax.dot_general(queries, keys, (((1,), (1,)), ((), ())), preferred_element_type=jnp.float32)


def row_top(blocks):
    best = blocks[0]
    for block in blocks[1:]:
        best = jnp.maximum(best, block)
    return jnp.max(best, axis=1, keepdims=True)


def row_sum(blocks):
    added = blocks[0]
    for block in blocks[1:]:
        added = added + block
    return jnp.sum(added, axis=1, keepdims=True)


def split(scores):
    return [scores[:, c : c + BLK] for c in range(0, scores.shape[1], BLK)]


def with_ones(values):
    return jnp.concatenate([values, jnp.ones_like(values)], axis=1)


def cases(count, most, body):
    for n in range(most + 1):
        pl.when(count == n)(functools.partial(body, n))


def first_kernel(cp_size, chunk, meta_ref, q_ref, own_ref, other_ref, keys_ref, values_ref, max_ref, acc_ref):
    half = meta_ref[1]
    reach = keys_ref.shape[0] // BLK
    count, same = extent(meta_ref, cp_size, half, reach)
    swap = half == 1
    mine, other = own_ref[...], other_ref[...]
    low, high = jnp.where(swap, other, mine), jnp.where(swap, mine, other)
    rows = lax.broadcasted_iota(jnp.int32, (BLK, BLK), 0)
    cols = lax.broadcasted_iota(jnp.int32, (BLK, BLK), 1)
    causal = jnp.where(cols <= rows, 0.0, NEGATIVE)
    causal = jnp.concatenate([causal] * chunk, axis=0)

    def attend(a, own, n):
        own_values = with_ones(own[:, HD:])
        for group in range(q_ref.shape[1] // (BLK * chunk)):
            at = slice(group * chunk * BLK, (group + 1) * chunk * BLK)
            queries = q_ref[a, at]
            blocks = split(score(queries, own[:, 0:HD]))
            blocks[-1] = blocks[-1] + causal
            if n:
                blocks = blocks + split(score(queries, keys_ref[0 : n * BLK, :]))
            top = row_top(blocks)
            weights = [jnp.exp2((block - top) * SCALE2).astype(jnp.bfloat16) for block in blocks]
            mid = own.shape[0] // BLK
            total = jnp.dot(
                jnp.concatenate(weights[:mid], axis=1), own_values, preferred_element_type=jnp.float32
            )
            if n:
                total = total + jnp.dot(
                    jnp.concatenate(weights[mid:], axis=1),
                    with_ones(values_ref[0 : n * BLK, :]),
                    preferred_element_type=jnp.float32,
                )
            max_ref[a, at] = jnp.broadcast_to(top, (chunk * BLK, HD))
            acc_ref[a, at] = total

    cases(count, reach, functools.partial(attend, 0, low))

    @pl.when(same)
    def _():
        cases(count, reach, functools.partial(attend, 1, jnp.concatenate([low, high], axis=0)))

    @pl.when(jnp.logical_not(same))
    def _():
        attend(1, high, 0)


def weigh_kernel(cp_size, chunk, meta_ref, q_ref, keys_ref, max_ref, acc_ref, weights_ref, rest_ref):
    reach = keys_ref.shape[0] // BLK
    count, same = extent(meta_ref, cp_size, 1 - meta_ref[1], reach)

    def weigh(a, n):
        for group in range(q_ref.shape[1] // (BLK * chunk)):
            at = slice(group * chunk * BLK, (group + 1) * chunk * BLK)
            old, total = acc_ref[a, at, 0:HD], acc_ref[a, at, HD:]
            if n:
                blocks = split(score(q_ref[a, at], keys_ref[0 : n * BLK, :]))
                old_top = max_ref[a, at]
                top = jnp.maximum(row_top(blocks), old_top)
                fade = jnp.exp2((old_top - top) * SCALE2)
                blocks = [jnp.exp2((block - top) * SCALE2) for block in blocks]
                share = 1.0 / (total * fade + row_sum(blocks))
                for index, block in enumerate(blocks):
                    weights_ref[a, at, index * BLK : (index + 1) * BLK] = (block * share).astype(jnp.bfloat16)
                rest_ref[a, at] = old * (fade * share)
            else:
                rest_ref[a, at] = old / total
            empty = reach - n
            if empty:
                weights_ref[a, at, n * BLK :] = jnp.zeros((chunk * BLK, empty * BLK), jnp.bfloat16)

    for a in range(2):
        cases(count if a == 0 else jnp.where(same, count, 0), reach, functools.partial(weigh, a))


def finish_kernel(chunk, weights_ref, rest_ref, values_ref, out_ref, done, sems):
    groups = rest_ref.shape[1] // (BLK * chunk)
    copies = []
    for a in range(2):
        for group in range(groups):
            at = slice(group * chunk * BLK, (group + 1) * chunk * BLK)
            result = rest_ref[a, at] + jnp.dot(
                weights_ref[a, at], values_ref[...], preferred_element_type=jnp.float32
            )
            result = result.astype(done.dtype)
            for h in range(chunk):
                done[a, group, :, h * HD : (h + 1) * HD] = result[h * BLK : (h + 1) * BLK]
            place = out_ref.at[pl.ds(a * BLK, BLK), pl.ds(group * chunk * HD, chunk * HD)]
            copies.append(pltpu.make_async_copy(done.at[a, group], place, sems.at[a, group]))
            copies[-1].start()
    for copy in copies:
        copy.wait()


VMEM = pl.BlockSpec(memory_space=pltpu.VMEM)
SMEM = pl.BlockSpec(memory_space=pltpu.SMEM)
ANY = pl.BlockSpec(memory_space=pl.ANY)


def local_call(kernel, name, outs, in_specs, grant, flops, **extra):
    return pl.pallas_call(
        kernel,
        out_shape=outs,
        in_specs=in_specs,
        compiler_params=pltpu.CompilerParams(vmem_limit_bytes=grant * 1024 * 1024),
        cost_estimate=pl.CostEstimate(flops=flops, bytes_accessed=1 << 20, transcendentals=0),
        name=name,
        **{"out_specs": [VMEM] * len(outs), **extra},
    )


def stack_queries(queries):
    heads = queries.shape[1] // HD
    outs = [jax.ShapeDtypeStruct((2, heads * BLK, HD), queries.dtype)]
    scratch = [pltpu.SemaphoreType.DMA((2, heads))]
    return local_call(stack_kernel, "stack_queries", outs, [ANY], 4, 1 << 20, scratch_shapes=scratch)(queries)[0]


def attend(cp_size, meta, queries, own, other, keys, values, other_keys, other_values):
    reach, rows = keys.shape[0] // BLK, queries.shape[1]
    chunk = min(rows // BLK, 4)
    groups = rows // (BLK * chunk)
    state = lambda width, dtype=jnp.float32: jax.ShapeDtypeStruct((2, rows, width), dtype)
    kernel = functools.partial(first_kernel, cp_size, chunk)
    outs, ins = [state(HD), state(2 * HD)], [SMEM] + [VMEM] * 5
    top, acc = local_call(kernel, "attend_first", outs, ins, 12, 1 << 31)(meta, queries, own, other, keys, values)
    kernel = functools.partial(weigh_kernel, cp_size, chunk)
    outs, ins = [state(reach * BLK, jnp.bfloat16), state(HD)], [SMEM] + [VMEM] * 4
    weights, rest = local_call(kernel, "attend_weigh", outs, ins, 12, 1 << 30)(meta, queries, other_keys, top, acc)
    outs = [jax.ShapeDtypeStruct((2 * BLK, rows // BLK * HD), queries.dtype)]
    scratch = [
        pltpu.VMEM((2, groups, BLK, chunk * HD), queries.dtype),
        pltpu.SemaphoreType.DMA((2, groups)),
    ]
    kernel = functools.partial(finish_kernel, chunk)
    finish = local_call(
        kernel, "attend_finish", outs, [VMEM] * 3, 8, 1 << 29, out_specs=[ANY], scratch_shapes=scratch
    )
    return finish(weights, rest, other_values)[0]


def shards(cp_size, sp_size, queries, keys, values, doc_ids, span_order):
    reach = doc_ids.shape[0] // 8
    staged = cp_size == 16 and sp_size == 2
    cp_index = lax.axis_index("cp").astype(jnp.int32)
    half = lax.axis_index("sp").astype(jnp.int32) if staged else jnp.int32(0)
    meta = jnp.concatenate([jnp.stack([cp_index, half]), span_order, doc_ids])
    own = lax.pad(keys, jnp.bfloat16(0), ((0, 0, 0), (0, HD, 0)))
    own = own + lax.pad(values, jnp.bfloat16(0), ((0, 0, 0), (HD, 0, 0)))
    queries = stack_queries(queries)
    if staged:
        by_x = lambda array: flip(array, "cp", cp_size, 2)
        by_y = lambda array: flip(array, "sp", sp_size, 1)
        by_core = lambda array: flip(array, "cp", cp_size, 1)
        far = {j: flip(own, "cp", cp_size, 4 * j) for j in (3, 2, 1)}
        far[0] = own
        other = by_y(own)
        sources = []
        for group in LINES:
            line = jnp.stack([far[j] for j in group])
            side, meta, other, queries = lax.optimization_barrier((by_x(line), meta, other, queries))
            sources += [line, side, by_core(line), by_core(side)]
        part = jax.ShapeDtypeStruct((reach * BLK, HD), jnp.bfloat16)
        picked = local_call(
            functools.partial(select_kernel, cp_size), "select", [part] * 2, [SMEM] + [VMEM] * len(sources), 4, 1 << 20
        )(meta, *sources)
        others = [by_y(array) for array in picked]
    else:
        pair = lax.all_gather(own, ("cp", "sp"), axis=0, tiled=True).reshape(cp_size, 2, BLK, 2, HD)
        holder = jnp.argsort(span_order)
        back = jnp.maximum(span_order[cp_index] - jnp.arange(reach + 1, dtype=jnp.int32), 0)
        chosen = pair[holder[back]]
        own, other = (chosen[0, k].reshape(BLK, 2 * HD) for k in (0, 1))
        picked, others = ([chosen[1:, k, :, part].reshape(reach * BLK, HD) for part in (0, 1)] for k in (0, 1))
    return attend(cp_size, meta, queries, own, other, *picked, *others)


def solution(mesh):
    in_specs = (P("cp", "sp"), P(("cp", "sp"), None), P(("cp", "sp"), None), P(), P())
    out_specs = P("cp", "sp")
    body = functools.partial(shards, mesh.shape["cp"], mesh.shape["sp"])
    return jax.shard_map(body, mesh=mesh, in_specs=in_specs, out_specs=out_specs, check_vma=False)
```

```python
import functools
import math

import jax
import jax.numpy as jnp
from jax import lax
from jax.experimental import pallas as pl
from jax.experimental.pallas import tpu as pltpu
from jax.sharding import PartitionSpec as P

HD = 128
SPAN = 256
BLK = 128
NEGATIVE = -1e30
HEAD = 2
SCALE2 = math.log2(math.e) / math.sqrt(HD)
LINES = ((3, 0), (1, 2))


def flip(array, axis, size, mask):
    return lax.ppermute(array, axis, [(i, i ^ mask) for i in range(size)])


def locate(apart):
    line = apart >> 2
    group = (line ^ (line >> 1)) & 1
    return group * 4 + (apart & 1) * 2 + ((apart >> 1) & 1), 1 - (line & 1)


def select_kernel(cp_size, meta_ref, *refs):
    sources, (keys_ref, values_ref) = refs[:-2], refs[-2:]
    cp = meta_ref[0]
    own_span = meta_ref[HEAD + cp]
    for back in range(1, keys_ref.shape[0] // BLK + 1):
        span = jnp.maximum(own_span - back, 0)
        holder = jnp.int32(0)
        for index in range(cp_size):
            holder = jnp.where(meta_ref[HEAD + index] == span, jnp.int32(index), holder)
        source, slot = locate(holder ^ cp)
        for index, ref in enumerate(sources):

            @pl.when(source == index)
            def _():
                rows = slice((back - 1) * BLK, back * BLK)
                keys_ref[rows, :] = ref[slot, :, 0:HD]
                values_ref[rows, :] = ref[slot, :, HD:]


def extent(meta_ref, cp_size, half, reach):
    span = meta_ref[HEAD + meta_ref[0]]
    doc_at = HEAD + cp_size
    doc = meta_ref[doc_at + 2 * span]
    count = jnp.int32(0)
    for back in range(1, reach + 1):
        block = 2 * (span - back) + half
        held = (block >= 0) & (meta_ref[doc_at + jnp.maximum(block, 0)] == doc)
        count = count + jnp.where(held, 1, 0)
    return count, doc == meta_ref[doc_at + 2 * span + 1]


def stack_kernel(q_ref, out_ref, sems):
    heads = out_ref.shape[1] // BLK
    copies = [
        pltpu.make_async_copy(
            q_ref.at[pl.ds(a * BLK, BLK), pl.ds(h * HD, HD)], out_ref.at[a, pl.ds(h * BLK, BLK), :], sems.at[a, h]
        )
        for a in range(2)
        for h in range(heads)
    ]
    for copy in copies:
        copy.start()
    for copy in copies:
        copy.wait()


def score(queries, keys):
    return lax.dot_general(queries, keys, (((1,), (1,)), ((), ())), preferred_element_type=jnp.float32)


def row_top(blocks):
    best = blocks[0]
    for block in blocks[1:]:
        best = jnp.maximum(best, block)
    return jnp.max(best, axis=1, keepdims=True)


def row_sum(blocks):
    added = blocks[0]
    for block in blocks[1:]:
        added = added + block
    return jnp.sum(added, axis=1, keepdims=True)


def split(scores):
    return [scores[:, c : c + BLK] for c in range(0, scores.shape[1], BLK)]


def with_ones(values):
    return jnp.concatenate([values, jnp.ones_like(values)], axis=1)


def cases(count, most, body):
    for n in range(most + 1):
        pl.when(count == n)(functools.partial(body, n))


def first_kernel(cp_size, chunk, meta_ref, q_ref, own_ref, other_ref, keys_ref, values_ref, max_ref, acc_ref):
    half = meta_ref[1]
    reach = keys_ref.shape[0] // BLK
    count, same = extent(meta_ref, cp_size, half, reach)
    swap = half == 1
    mine, other = own_ref[...], other_ref[...]
    low, high = jnp.where(swap, other, mine), jnp.where(swap, mine, other)
    rows = lax.broadcasted_iota(jnp.int32, (BLK, BLK), 0)
    cols = lax.broadcasted_iota(jnp.int32, (BLK, BLK), 1)
    causal = jnp.where(cols <= rows, 0.0, NEGATIVE)
    causal = jnp.concatenate([causal] * chunk, axis=0)

    def attend(a, own, n):
        own_values = with_ones(own[:, HD:])
        for group in range(q_ref.shape[1] // (BLK * chunk)):
            at = slice(group * chunk * BLK, (group + 1) * chunk * BLK)
            queries = q_ref[a, at]
            blocks = split(score(queries, own[:, 0:HD]))
            blocks[-1] = blocks[-1] + causal
            if n:
                blocks = blocks + split(score(queries, keys_ref[0 : n * BLK, :]))
            top = row_top(blocks)
            weights = [jnp.exp2((block - top) * SCALE2).astype(jnp.bfloat16) for block in blocks]
            mid = own.shape[0] // BLK
            total = jnp.dot(
                jnp.concatenate(weights[:mid], axis=1), own_values, preferred_element_type=jnp.float32
            )
            if n:
                total = total + jnp.dot(
                    jnp.concatenate(weights[mid:], axis=1),
                    with_ones(values_ref[0 : n * BLK, :]),
                    preferred_element_type=jnp.float32,
                )
            max_ref[a, at] = jnp.broadcast_to(top, (chunk * BLK, HD))
            acc_ref[a, at] = total

    cases(count, reach, functools.partial(attend, 0, low))

    @pl.when(same)
    def _():
        cases(count, reach, functools.partial(attend, 1, jnp.concatenate([low, high], axis=0)))

    @pl.when(jnp.logical_not(same))
    def _():
        attend(1, high, 0)


def weigh_kernel(cp_size, chunk, meta_ref, q_ref, keys_ref, max_ref, acc_ref, weights_ref, rest_ref):
    reach = keys_ref.shape[0] // BLK
    count, same = extent(meta_ref, cp_size, 1 - meta_ref[1], reach)

    def weigh(a, n):
        for group in range(q_ref.shape[1] // (BLK * chunk)):
            at = slice(group * chunk * BLK, (group + 1) * chunk * BLK)
            old, total = acc_ref[a, at, 0:HD], acc_ref[a, at, HD:]
            if n:
                blocks = split(score(q_ref[a, at], keys_ref[0 : n * BLK, :]))
                old_top = max_ref[a, at]
                top = jnp.maximum(row_top(blocks), old_top)
                fade = jnp.exp2((old_top - top) * SCALE2)
                blocks = [jnp.exp2((block - top) * SCALE2) for block in blocks]
                share = 1.0 / (total * fade + row_sum(blocks))
                for index, block in enumerate(blocks):
                    weights_ref[a, at, index * BLK : (index + 1) * BLK] = (block * share).astype(jnp.bfloat16)
                rest_ref[a, at] = old * (fade * share)
            else:
                rest_ref[a, at] = old / total
            empty = reach - n
            if empty:
                weights_ref[a, at, n * BLK :] = jnp.zeros((chunk * BLK, empty * BLK), jnp.bfloat16)

    for a in range(2):
        cases(count if a == 0 else jnp.where(same, count, 0), reach, functools.partial(weigh, a))


def finish_kernel(chunk, weights_ref, rest_ref, values_ref, out_ref, done, sems):
    groups = rest_ref.shape[1] // (BLK * chunk)
    copies = []
    for a in range(2):
        for group in range(groups):
            at = slice(group * chunk * BLK, (group + 1) * chunk * BLK)
            result = rest_ref[a, at] + jnp.dot(
                weights_ref[a, at], values_ref[...], preferred_element_type=jnp.float32
            )
            result = result.astype(done.dtype)
            for h in range(chunk):
                done[a, group, :, h * HD : (h + 1) * HD] = result[h * BLK : (h + 1) * BLK]
            place = out_ref.at[pl.ds(a * BLK, BLK), pl.ds(group * chunk * HD, chunk * HD)]
            copies.append(pltpu.make_async_copy(done.at[a, group], place, sems.at[a, group]))
            copies[-1].start()
    for copy in copies:
        copy.wait()


VMEM = pl.BlockSpec(memory_space=pltpu.VMEM)
SMEM = pl.BlockSpec(memory_space=pltpu.SMEM)
ANY = pl.BlockSpec(memory_space=pl.ANY)


def local_call(kernel, name, outs, in_specs, grant, flops, **extra):
    return pl.pallas_call(
        kernel,
        out_shape=outs,
        in_specs=in_specs,
        compiler_params=pltpu.CompilerParams(vmem_limit_bytes=grant * 1024 * 1024),
        cost_estimate=pl.CostEstimate(flops=flops, bytes_accessed=1 << 20, transcendentals=0),
        name=name,
        **{"out_specs": [VMEM] * len(outs), **extra},
    )


def stack_queries(queries):
    heads = queries.shape[1] // HD
    outs = [jax.ShapeDtypeStruct((2, heads * BLK, HD), queries.dtype)]
    scratch = [pltpu.SemaphoreType.DMA((2, heads))]
    return local_call(stack_kernel, "stack_queries", outs, [ANY], 4, 1 << 20, scratch_shapes=scratch)(queries)[0]


def attend(cp_size, meta, queries, own, other, keys, values, other_keys, other_values):
    reach, rows = keys.shape[0] // BLK, queries.shape[1]
    chunk = min(rows // BLK, 4)
    groups = rows // (BLK * chunk)
    state = lambda width, dtype=jnp.float32: jax.ShapeDtypeStruct((2, rows, width), dtype)
    kernel = functools.partial(first_kernel, cp_size, chunk)
    outs, ins = [state(HD), state(2 * HD)], [SMEM] + [VMEM] * 5
    top, acc = local_call(kernel, "attend_first", outs, ins, 12, 1 << 31)(meta, queries, own, other, keys, values)
    kernel = functools.partial(weigh_kernel, cp_size, chunk)
    outs, ins = [state(reach * BLK, jnp.bfloat16), state(HD)], [SMEM] + [VMEM] * 4
    weights, rest = local_call(kernel, "attend_weigh", outs, ins, 12, 1 << 30)(meta, queries, other_keys, top, acc)
    outs = [jax.ShapeDtypeStruct((2 * BLK, rows // BLK * HD), queries.dtype)]
    scratch = [
        pltpu.VMEM((2, groups, BLK, chunk * HD), queries.dtype),
        pltpu.SemaphoreType.DMA((2, groups)),
    ]
    kernel = functools.partial(finish_kernel, chunk)
    finish = local_call(
        kernel, "attend_finish", outs, [VMEM] * 3, 8, 1 << 29, out_specs=[ANY], scratch_shapes=scratch
    )
    return finish(weights, rest, other_values)[0]


def shards(cp_size, sp_size, queries, keys, values, doc_ids, span_order):
    reach = doc_ids.shape[0] // 8
    staged = cp_size == 16 and sp_size == 2
    cp_index = lax.axis_index("cp").astype(jnp.int32)
    half = lax.axis_index("sp").astype(jnp.int32) if staged else jnp.int32(0)
    meta = jnp.concatenate([jnp.stack([cp_index, half]), span_order, doc_ids])
    own = lax.pad(keys, jnp.bfloat16(0), ((0, 0, 0), (0, HD, 0)))
    own = own + lax.pad(values, jnp.bfloat16(0), ((0, 0, 0), (HD, 0, 0)))
    queries = stack_queries(queries)
    if staged:
        by_x = lambda array: flip(array, "cp", cp_size, 2)
        by_y = lambda array: flip(array, "sp", sp_size, 1)
        by_core = lambda array: flip(array, "cp", cp_size, 1)
        far = {j: flip(own, "cp", cp_size, 4 * j) for j in (3, 2, 1)}
        far[1], far[2], queries, meta = lax.optimization_barrier((far[1], far[2], queries, meta))
        far[0] = own
        sources = []
        for group in LINES:
            line = jnp.stack([far[j] for j in group])
            side = by_x(line)
            sources += [line, side, by_core(line), by_core(side)]
        sources[5], own_late = lax.optimization_barrier((sources[5], own))
        other = by_y(own_late)
        part = jax.ShapeDtypeStruct((reach * BLK, HD), jnp.bfloat16)
        picked = local_call(
            functools.partial(select_kernel, cp_size), "select", [part] * 2, [SMEM] + [VMEM] * len(sources), 4, 1 << 20
        )(meta, *sources)
        others = [by_y(array) for array in picked]
    else:
        pair = lax.all_gather(own, ("cp", "sp"), axis=0, tiled=True).reshape(cp_size, 2, BLK, 2, HD)
        holder = jnp.argsort(span_order)
        back = jnp.maximum(span_order[cp_index] - jnp.arange(reach + 1, dtype=jnp.int32), 0)
        chosen = pair[holder[back]]
        own, other = (chosen[0, k].reshape(BLK, 2 * HD) for k in (0, 1))
        picked, others = ([chosen[1:, k, :, part].reshape(reach * BLK, HD) for part in (0, 1)] for k in (0, 1))
    return attend(cp_size, meta, queries, own, other, *picked, *others)


def solution(mesh):
    in_specs = (P("cp", "sp"), P(("cp", "sp"), None), P(("cp", "sp"), None), P(), P())
    out_specs = P("cp", "sp")
    body = functools.partial(shards, mesh.shape["cp"], mesh.shape["sp"])
    return jax.shard_map(body, mesh=mesh, in_specs=in_specs, out_specs=out_specs, check_vma=False)
```

```python
import functools
import math

import jax
import jax.numpy as jnp
from jax import lax
from jax.experimental import pallas as pl
from jax.experimental.pallas import tpu as pltpu
from jax.sharding import PartitionSpec as P

HD = 128
SPAN = 256
BLK = 128
NEGATIVE = -1e30
HEAD = 2
SCALE2 = math.log2(math.e) / math.sqrt(HD)
LINES = ((3, 0), (1, 2))


def flip(array, axis, size, mask):
    return lax.ppermute(array, axis, [(i, i ^ mask) for i in range(size)])


def locate(apart):
    line = apart >> 2
    group = (line ^ (line >> 1)) & 1
    return group * 4 + (apart & 1) * 2 + ((apart >> 1) & 1), 1 - (line & 1)


def select_kernel(cp_size, meta_ref, *refs):
    sources, (keys_ref, values_ref) = refs[:-2], refs[-2:]
    cp = meta_ref[0, 0]
    order = [meta_ref[0, HEAD + index] for index in range(cp_size)]
    own_span = jnp.int32(0)
    for index in range(cp_size):
        own_span = jnp.where(cp == index, order[index], own_span)
    for back in range(1, keys_ref.shape[0] // BLK + 1):
        span = jnp.maximum(own_span - back, 0)
        holder = jnp.int32(0)
        for index in range(cp_size):
            holder = jnp.where(order[index] == span, jnp.int32(index), holder)
        source, slot = locate(holder ^ cp)
        for index, ref in enumerate(sources):

            @pl.when(source == index)
            def _():
                rows = slice((back - 1) * BLK, back * BLK)
                keys_ref[rows, :] = ref[slot, :, 0:HD]
                values_ref[rows, :] = ref[slot, :, HD:]


def extent(meta_ref, cp_size, half, reach):
    span = meta_ref[HEAD + meta_ref[0]]
    doc_at = HEAD + cp_size
    doc = meta_ref[doc_at + 2 * span]
    count = jnp.int32(0)
    for back in range(1, reach + 1):
        block = 2 * (span - back) + half
        held = (block >= 0) & (meta_ref[doc_at + jnp.maximum(block, 0)] == doc)
        count = count + jnp.where(held, 1, 0)
    return count, doc == meta_ref[doc_at + 2 * span + 1]


def stack_kernel(q_ref, out_ref, sems):
    heads = out_ref.shape[1] // BLK
    copies = [
        pltpu.make_async_copy(
            q_ref.at[pl.ds(a * BLK, BLK), pl.ds(h * HD, HD)], out_ref.at[a, pl.ds(h * BLK, BLK), :], sems.at[a, h]
        )
        for a in range(2)
        for h in range(heads)
    ]
    for copy in copies:
        copy.start()
    for copy in copies:
        copy.wait()


def score(queries, keys):
    return lax.dot_general(queries, keys, (((1,), (1,)), ((), ())), preferred_element_type=jnp.float32)


def row_top(blocks):
    best = blocks[0]
    for block in blocks[1:]:
        best = jnp.maximum(best, block)
    return jnp.max(best, axis=1, keepdims=True)


def row_sum(blocks):
    added = blocks[0]
    for block in blocks[1:]:
        added = added + block
    return jnp.sum(added, axis=1, keepdims=True)


def split(scores):
    return [scores[:, c : c + BLK] for c in range(0, scores.shape[1], BLK)]


def with_ones(values):
    return jnp.concatenate([values, jnp.ones_like(values)], axis=1)


def cases(count, most, body):
    for n in range(most + 1):
        pl.when(count == n)(functools.partial(body, n))


def first_kernel(cp_size, chunk, meta_ref, q_ref, own_ref, other_ref, keys_ref, values_ref, max_ref, acc_ref, plan_ref):
    half = meta_ref[1]
    reach = keys_ref.shape[0] // BLK
    count, same = extent(meta_ref, cp_size, half, reach)
    beyond, same = extent(meta_ref, cp_size, 1 - half, reach)
    plan_ref[0:1, :] = jnp.full((1, HD), beyond, jnp.int32)
    plan_ref[1:2, :] = jnp.full((1, HD), jnp.where(same, 1, 0), jnp.int32)
    swap = half == 1
    mine, other = own_ref[...], other_ref[...]
    low, high = jnp.where(swap, other, mine), jnp.where(swap, mine, other)
    rows = lax.broadcasted_iota(jnp.int32, (BLK, BLK), 0)
    cols = lax.broadcasted_iota(jnp.int32, (BLK, BLK), 1)
    causal = jnp.where(cols <= rows, 0.0, NEGATIVE)
    causal = jnp.concatenate([causal] * chunk, axis=0)

    def attend(a, own, n):
        own_values = with_ones(own[:, HD:])
        for group in range(q_ref.shape[1] // (BLK * chunk)):
            at = slice(group * chunk * BLK, (group + 1) * chunk * BLK)
            queries = q_ref[a, at]
            blocks = split(score(queries, own[:, 0:HD]))
            blocks[-1] = blocks[-1] + causal
            if n:
                blocks = blocks + split(score(queries, keys_ref[0 : n * BLK, :]))
            top = row_top(blocks)
            weights = [jnp.exp2((block - top) * SCALE2).astype(jnp.bfloat16) for block in blocks]
            mid = own.shape[0] // BLK
            total = jnp.dot(
                jnp.concatenate(weights[:mid], axis=1), own_values, preferred_element_type=jnp.float32
            )
            if n:
                total = total + jnp.dot(
                    jnp.concatenate(weights[mid:], axis=1),
                    with_ones(values_ref[0 : n * BLK, :]),
                    preferred_element_type=jnp.float32,
                )
            max_ref[a, at] = jnp.broadcast_to(top, (chunk * BLK, HD))
            acc_ref[a, at] = total

    cases(count, reach, functools.partial(attend, 0, low))

    @pl.when(same)
    def _():
        cases(count, reach, functools.partial(attend, 1, jnp.concatenate([low, high], axis=0)))

    @pl.when(jnp.logical_not(same))
    def _():
        attend(1, high, 0)


def weigh_kernel(chunk, plan_ref, q_ref, keys_ref, max_ref, acc_ref, weights_ref, rest_ref):
    reach = keys_ref.shape[0] // BLK
    count, same = plan_ref[0, 0], plan_ref[1, 0] == 1

    def weigh(a, n):
        for group in range(q_ref.shape[1] // (BLK * chunk)):
            at = slice(group * chunk * BLK, (group + 1) * chunk * BLK)
            old, total = acc_ref[a, at, 0:HD], acc_ref[a, at, HD:]
            if n:
                blocks = split(score(q_ref[a, at], keys_ref[0 : n * BLK, :]))
                old_top = max_ref[a, at]
                top = jnp.maximum(row_top(blocks), old_top)
                fade = jnp.exp2((old_top - top) * SCALE2)
                blocks = [jnp.exp2((block - top) * SCALE2) for block in blocks]
                share = 1.0 / (total * fade + row_sum(blocks))
                for index, block in enumerate(blocks):
                    weights_ref[a, at, index * BLK : (index + 1) * BLK] = (block * share).astype(jnp.bfloat16)
                rest_ref[a, at] = old * (fade * share)
            else:
                rest_ref[a, at] = old / total
            empty = reach - n
            if empty:
                weights_ref[a, at, n * BLK :] = jnp.zeros((chunk * BLK, empty * BLK), jnp.bfloat16)

    for a in range(2):
        cases(count if a == 0 else jnp.where(same, count, 0), reach, functools.partial(weigh, a))


def finish_kernel(chunk, weights_ref, rest_ref, values_ref, out_ref, done, sems):
    groups = rest_ref.shape[1] // (BLK * chunk)
    copies = []
    for a in range(2):
        for group in range(groups):
            at = slice(group * chunk * BLK, (group + 1) * chunk * BLK)
            result = rest_ref[a, at] + jnp.dot(
                weights_ref[a, at], values_ref[...], preferred_element_type=jnp.float32
            )
            result = result.astype(done.dtype)
            for h in range(chunk):
                done[a, group, :, h * HD : (h + 1) * HD] = result[h * BLK : (h + 1) * BLK]
            place = out_ref.at[pl.ds(a * BLK, BLK), pl.ds(group * chunk * HD, chunk * HD)]
            copies.append(pltpu.make_async_copy(done.at[a, group], place, sems.at[a, group]))
            copies[-1].start()
    for copy in copies:
        copy.wait()


VMEM = pl.BlockSpec(memory_space=pltpu.VMEM)
SMEM = pl.BlockSpec(memory_space=pltpu.SMEM)
ANY = pl.BlockSpec(memory_space=pl.ANY)


def local_call(kernel, name, outs, in_specs, grant, flops, **extra):
    return pl.pallas_call(
        kernel,
        out_shape=outs,
        in_specs=in_specs,
        compiler_params=pltpu.CompilerParams(vmem_limit_bytes=grant * 1024 * 1024),
        cost_estimate=pl.CostEstimate(flops=flops, bytes_accessed=1 << 20, transcendentals=0),
        name=name,
        **{"out_specs": [VMEM] * len(outs), **extra},
    )


def stack_queries(queries):
    heads = queries.shape[1] // HD
    outs = [jax.ShapeDtypeStruct((2, heads * BLK, HD), queries.dtype)]
    scratch = [pltpu.SemaphoreType.DMA((2, heads))]
    return local_call(stack_kernel, "stack_queries", outs, [ANY], 4, 1 << 20, scratch_shapes=scratch)(queries)[0]


def attend(cp_size, meta, queries, own, other, keys, values, other_keys, other_values):
    reach, rows = keys.shape[0] // BLK, queries.shape[1]
    chunk = min(rows // BLK, 4)
    groups = rows // (BLK * chunk)
    state = lambda width, dtype=jnp.float32: jax.ShapeDtypeStruct((2, rows, width), dtype)
    kernel = functools.partial(first_kernel, cp_size, chunk)
    outs = [state(HD), state(2 * HD), jax.ShapeDtypeStruct((8, HD), jnp.int32)]
    ins = [SMEM] + [VMEM] * 5
    first = local_call(kernel, "attend_first", outs, ins, 12, 1 << 31)
    top, acc, plan = first(meta, queries, own, other, keys, values)
    kernel = functools.partial(weigh_kernel, chunk)
    outs, ins = [state(reach * BLK, jnp.bfloat16), state(HD)], [VMEM] * 5
    weights, rest = local_call(kernel, "attend_weigh", outs, ins, 12, 1 << 30)(plan, queries, other_keys, top, acc)
    outs = [jax.ShapeDtypeStruct((2 * BLK, rows // BLK * HD), queries.dtype)]
    scratch = [
        pltpu.VMEM((2, groups, BLK, chunk * HD), queries.dtype),
        pltpu.SemaphoreType.DMA((2, groups)),
    ]
    kernel = functools.partial(finish_kernel, chunk)
    finish = local_call(
        kernel, "attend_finish", outs, [VMEM] * 3, 8, 1 << 29, out_specs=[ANY], scratch_shapes=scratch
    )
    return finish(weights, rest, other_values)[0]


def shards(cp_size, sp_size, queries, keys, values, doc_ids, span_order):
    reach = doc_ids.shape[0] // 8
    staged = cp_size == 16 and sp_size == 2
    cp_index = lax.axis_index("cp").astype(jnp.int32)
    half = lax.axis_index("sp").astype(jnp.int32) if staged else jnp.int32(0)
    meta = jnp.concatenate([jnp.stack([cp_index, half]), span_order, doc_ids])
    own = lax.pad(keys, jnp.bfloat16(0), ((0, 0, 0), (0, HD, 0)))
    own = own + lax.pad(values, jnp.bfloat16(0), ((0, 0, 0), (HD, 0, 0)))
    queries = stack_queries(queries)
    if staged:
        by_x = lambda array: flip(array, "cp", cp_size, 2)
        by_y = lambda array: flip(array, "sp", sp_size, 1)
        by_core = lambda array: flip(array, "cp", cp_size, 1)
        far = {j: flip(own, "cp", cp_size, 4 * j) for j in (3, 2, 1)}
        far[1], far[2], queries, meta = lax.optimization_barrier((far[1], far[2], queries, meta))
        far[0] = own
        sources = []
        for group in LINES:
            line = jnp.stack([far[j] for j in group])
            side = by_x(line)
            sources += [line, side, by_core(line), by_core(side)]
        sources[5], own_late = lax.optimization_barrier((sources[5], own))
        other = by_y(own_late)
        part = jax.ShapeDtypeStruct((reach * BLK, HD), jnp.bfloat16)
        picked = local_call(
            functools.partial(select_kernel, cp_size), "select", [part] * 2, [VMEM] * (1 + len(sources)), 4, 1 << 20
        )(meta[None], *sources)
        others = [by_y(array) for array in picked]
    else:
        pair = lax.all_gather(own, ("cp", "sp"), axis=0, tiled=True).reshape(cp_size, 2, BLK, 2, HD)
        holder = jnp.argsort(span_order)
        back = jnp.maximum(span_order[cp_index] - jnp.arange(reach + 1, dtype=jnp.int32), 0)
        chosen = pair[holder[back]]
        own, other = (chosen[0, k].reshape(BLK, 2 * HD) for k in (0, 1))
        picked, others = ([chosen[1:, k, :, part].reshape(reach * BLK, HD) for part in (0, 1)] for k in (0, 1))
    return attend(cp_size, meta, queries, own, other, *picked, *others)


def solution(mesh):
    in_specs = (P("cp", "sp"), P(("cp", "sp"), None), P(("cp", "sp"), None), P(), P())
    out_specs = P("cp", "sp")
    body = functools.partial(shards, mesh.shape["cp"], mesh.shape["sp"])
    return jax.shard_map(body, mesh=mesh, in_specs=in_specs, out_specs=out_specs, check_vma=False)
```

```python
import functools
import math

import jax
import jax.numpy as jnp
from jax import lax
from jax.experimental import pallas as pl
from jax.experimental.pallas import tpu as pltpu
from jax.sharding import PartitionSpec as P

HD = 128
SPAN = 256
BLK = 128
NEGATIVE = -1e30
HEAD = 2
SCALE2 = math.log2(math.e) / math.sqrt(HD)
LINES = ((3, 0), (1, 2))


def flip(array, axis, size, mask):
    return lax.ppermute(array, axis, [(i, i ^ mask) for i in range(size)])


def locate(apart):
    line = apart >> 2
    group = (line ^ (line >> 1)) & 1
    return group * 4 + (apart & 1) * 2 + ((apart >> 1) & 1), 1 - (line & 1)


def select_kernel(cp_size, meta_ref, *refs):
    sources, (keys_ref, values_ref) = refs[:-2], refs[-2:]
    cp = meta_ref[0, 0]
    order = [meta_ref[0, HEAD + index] for index in range(cp_size)]
    own_span = jnp.int32(0)
    for index in range(cp_size):
        own_span = jnp.where(cp == index, order[index], own_span)
    for back in range(1, keys_ref.shape[0] // BLK + 1):
        span = jnp.maximum(own_span - back, 0)
        holder = jnp.int32(0)
        for index in range(cp_size):
            holder = jnp.where(order[index] == span, jnp.int32(index), holder)
        source, slot = locate(holder ^ cp)
        for index, ref in enumerate(sources):

            @pl.when(source == index)
            def _():
                rows = slice((back - 1) * BLK, back * BLK)
                keys_ref[rows, :] = ref[slot, :, 0:HD]
                values_ref[rows, :] = ref[slot, :, HD:]


def extent(meta_ref, cp_size, half, reach):
    span = meta_ref[HEAD + meta_ref[0]]
    doc_at = HEAD + cp_size
    doc = meta_ref[doc_at + 2 * span]
    count = jnp.int32(0)
    for back in range(1, reach + 1):
        block = 2 * (span - back) + half
        held = (block >= 0) & (meta_ref[doc_at + jnp.maximum(block, 0)] == doc)
        count = count + jnp.where(held, 1, 0)
    return count, doc == meta_ref[doc_at + 2 * span + 1]


def stack_kernel(q_ref, out_ref, sems):
    heads = out_ref.shape[1] // BLK
    copies = [
        pltpu.make_async_copy(
            q_ref.at[pl.ds(a * BLK, BLK), pl.ds(h * HD, HD)], out_ref.at[a, pl.ds(h * BLK, BLK), :], sems.at[a, h]
        )
        for a in range(2)
        for h in range(heads)
    ]
    for copy in copies:
        copy.start()
    for copy in copies:
        copy.wait()


def score(queries, keys):
    return lax.dot_general(queries, keys, (((1,), (1,)), ((), ())), preferred_element_type=jnp.float32)


def row_top(blocks):
    best = blocks[0]
    for block in blocks[1:]:
        best = jnp.maximum(best, block)
    return jnp.max(best, axis=1, keepdims=True)


def row_sum(blocks):
    added = blocks[0]
    for block in blocks[1:]:
        added = added + block
    return jnp.sum(added, axis=1, keepdims=True)


def split(scores):
    return [scores[:, c : c + BLK] for c in range(0, scores.shape[1], BLK)]


def with_ones(values):
    return jnp.concatenate([values, jnp.ones_like(values)], axis=1)


def cases(count, most, body):
    for n in range(most + 1):
        pl.when(count == n)(functools.partial(body, n))


def first_kernel(cp_size, chunk, meta_ref, q_ref, own_ref, other_ref, keys_ref, values_ref, max_ref, acc_ref, plan_ref):
    half = meta_ref[1]
    reach = keys_ref.shape[0] // BLK
    count, same = extent(meta_ref, cp_size, half, reach)
    beyond, same = extent(meta_ref, cp_size, 1 - half, reach)
    plan_ref[0:1, :] = jnp.full((1, HD), beyond, jnp.int32)
    plan_ref[1:2, :] = jnp.full((1, HD), jnp.where(same, 1, 0), jnp.int32)
    swap = half == 1
    mine, other = own_ref[...], other_ref[...]
    low, high = jnp.where(swap, other, mine), jnp.where(swap, mine, other)
    rows = lax.broadcasted_iota(jnp.int32, (BLK, BLK), 0)
    cols = lax.broadcasted_iota(jnp.int32, (BLK, BLK), 1)
    causal = jnp.where(cols <= rows, 0.0, NEGATIVE)
    causal = jnp.concatenate([causal] * chunk, axis=0)

    def attend(a, own, n):
        own_values = with_ones(own[:, HD:])
        for group in range(q_ref.shape[1] // (BLK * chunk)):
            at = slice(group * chunk * BLK, (group + 1) * chunk * BLK)
            queries = q_ref[a, at]
            blocks = split(score(queries, own[:, 0:HD]))
            blocks[-1] = blocks[-1] + causal
            if n:
                blocks = blocks + split(score(queries, keys_ref[0 : n * BLK, :]))
            top = row_top(blocks)
            weights = [jnp.exp2((block - top) * SCALE2).astype(jnp.bfloat16) for block in blocks]
            mid = own.shape[0] // BLK
            total = jnp.dot(
                jnp.concatenate(weights[:mid], axis=1), own_values, preferred_element_type=jnp.float32
            )
            if n:
                total = total + jnp.dot(
                    jnp.concatenate(weights[mid:], axis=1),
                    with_ones(values_ref[0 : n * BLK, :]),
                    preferred_element_type=jnp.float32,
                )
            max_ref[a, at] = jnp.broadcast_to(top, (chunk * BLK, HD))
            acc_ref[a, at] = total

    cases(count, reach, functools.partial(attend, 0, low))

    @pl.when(same)
    def _():
        cases(count, reach, functools.partial(attend, 1, jnp.concatenate([low, high], axis=0)))

    @pl.when(jnp.logical_not(same))
    def _():
        attend(1, high, 0)


def weigh_kernel(chunk, plan_ref, q_ref, keys_ref, max_ref, acc_ref, weights_ref, rest_ref):
    reach = keys_ref.shape[0] // BLK
    count, same = plan_ref[0, 0], plan_ref[1, 0] == 1

    def weigh(a, n):
        for group in range(q_ref.shape[1] // (BLK * chunk)):
            at = slice(group * chunk * BLK, (group + 1) * chunk * BLK)
            old, total = acc_ref[a, at, 0:HD], acc_ref[a, at, HD:]
            if n:
                blocks = split(score(q_ref[a, at], keys_ref[0 : n * BLK, :]))
                old_top = max_ref[a, at]
                top = jnp.maximum(row_top(blocks), old_top)
                fade = jnp.exp2((old_top - top) * SCALE2)
                blocks = [jnp.exp2((block - top) * SCALE2) for block in blocks]
                share = 1.0 / (total * fade + row_sum(blocks))
                for index, block in enumerate(blocks):
                    weights_ref[a, at, index * BLK : (index + 1) * BLK] = (block * share).astype(jnp.bfloat16)
                rest_ref[a, at] = old * (fade * share)
            else:
                rest_ref[a, at] = old / total
            empty = reach - n
            if empty:
                weights_ref[a, at, n * BLK :] = jnp.zeros((chunk * BLK, empty * BLK), jnp.bfloat16)

    for a in range(2):
        cases(count if a == 0 else jnp.where(same, count, 0), reach, functools.partial(weigh, a))


def finish_kernel(chunk, plan_ref, weights_ref, rest_ref, values_ref, out_ref, done, sems):
    reach = values_ref.shape[0] // BLK
    groups = rest_ref.shape[1] // (BLK * chunk)
    places = [(a, group) for a in range(2) for group in range(groups)]
    copies = [
        pltpu.make_async_copy(
            done.at[a, group],
            out_ref.at[pl.ds(a * BLK, BLK), pl.ds(group * chunk * HD, chunk * HD)],
            sems.at[a, group],
        )
        for a, group in places
    ]

    def finish(pairs):
        depth = min(2 * pairs, reach) * BLK
        for (a, group), copy in zip(places, copies):
            at = slice(group * chunk * BLK, (group + 1) * chunk * BLK)
            result = rest_ref[a, at]
            if depth:
                result = result + jnp.dot(
                    weights_ref[a, at, 0:depth], values_ref[0:depth, :], preferred_element_type=jnp.float32
                )
            result = result.astype(done.dtype)
            for h in range(chunk):
                done[a, group, :, h * HD : (h + 1) * HD] = result[h * BLK : (h + 1) * BLK]
            copy.start()
        for copy in copies:
            copy.wait()

    cases((plan_ref[0, 0] + 1) // 2, (reach + 1) // 2, finish)


VMEM = pl.BlockSpec(memory_space=pltpu.VMEM)
SMEM = pl.BlockSpec(memory_space=pltpu.SMEM)
ANY = pl.BlockSpec(memory_space=pl.ANY)


def local_call(kernel, name, outs, in_specs, grant, flops, **extra):
    return pl.pallas_call(
        kernel,
        out_shape=outs,
        in_specs=in_specs,
        compiler_params=pltpu.CompilerParams(vmem_limit_bytes=grant * 1024 * 1024),
        cost_estimate=pl.CostEstimate(flops=flops, bytes_accessed=1 << 20, transcendentals=0),
        name=name,
        **{"out_specs": [VMEM] * len(outs), **extra},
    )


def stack_queries(queries):
    heads = queries.shape[1] // HD
    outs = [jax.ShapeDtypeStruct((2, heads * BLK, HD), queries.dtype)]
    scratch = [pltpu.SemaphoreType.DMA((2, heads))]
    return local_call(stack_kernel, "stack_queries", outs, [ANY], 4, 1 << 20, scratch_shapes=scratch)(queries)[0]


def attend(cp_size, meta, queries, own, other, keys, values, other_keys, other_values):
    reach, rows = keys.shape[0] // BLK, queries.shape[1]
    chunk = min(rows // BLK, 4)
    groups = rows // (BLK * chunk)
    state = lambda width, dtype=jnp.float32: jax.ShapeDtypeStruct((2, rows, width), dtype)
    kernel = functools.partial(first_kernel, cp_size, chunk)
    outs = [state(HD), state(2 * HD), jax.ShapeDtypeStruct((8, HD), jnp.int32)]
    ins = [SMEM] + [VMEM] * 5
    first = local_call(kernel, "attend_first", outs, ins, 12, 1 << 31)
    top, acc, plan = first(meta, queries, own, other, keys, values)
    kernel = functools.partial(weigh_kernel, chunk)
    outs, ins = [state(reach * BLK, jnp.bfloat16), state(HD)], [VMEM] * 5
    weights, rest = local_call(kernel, "attend_weigh", outs, ins, 12, 1 << 30)(plan, queries, other_keys, top, acc)
    outs = [jax.ShapeDtypeStruct((2 * BLK, rows // BLK * HD), queries.dtype)]
    scratch = [
        pltpu.VMEM((2, groups, BLK, chunk * HD), queries.dtype),
        pltpu.SemaphoreType.DMA((2, groups)),
    ]
    kernel = functools.partial(finish_kernel, chunk)
    finish = local_call(
        kernel, "attend_finish", outs, [VMEM] * 4, 8, 1 << 29, out_specs=[ANY], scratch_shapes=scratch
    )
    return finish(plan, weights, rest, other_values)[0]


def shards(cp_size, sp_size, queries, keys, values, doc_ids, span_order):
    reach = doc_ids.shape[0] // 8
    staged = cp_size == 16 and sp_size == 2
    cp_index = lax.axis_index("cp").astype(jnp.int32)
    half = lax.axis_index("sp").astype(jnp.int32) if staged else jnp.int32(0)
    meta = jnp.concatenate([jnp.stack([cp_index, half]), span_order, doc_ids])
    own = lax.pad(keys, jnp.bfloat16(0), ((0, 0, 0), (0, HD, 0)))
    own = own + lax.pad(values, jnp.bfloat16(0), ((0, 0, 0), (HD, 0, 0)))
    queries = stack_queries(queries)
    if staged:
        by_x = lambda array: flip(array, "cp", cp_size, 2)
        by_y = lambda array: flip(array, "sp", sp_size, 1)
        by_core = lambda array: flip(array, "cp", cp_size, 1)
        far = {j: flip(own, "cp", cp_size, 4 * j) for j in (3, 2, 1)}
        far[1], far[2], queries, meta = lax.optimization_barrier((far[1], far[2], queries, meta))
        far[0] = own
        sources = []
        for group in LINES:
            line = jnp.stack([far[j] for j in group])
            side = by_x(line)
            sources += [line, side, by_core(line), by_core(side)]
        sources[5], own_late = lax.optimization_barrier((sources[5], own))
        other = by_y(own_late)
        part = jax.ShapeDtypeStruct((reach * BLK, HD), jnp.bfloat16)
        picked = local_call(
            functools.partial(select_kernel, cp_size), "select", [part] * 2, [VMEM] * (1 + len(sources)), 4, 1 << 20
        )(meta[None], *sources)
        others = [by_y(array) for array in picked]
    else:
        pair = lax.all_gather(own, ("cp", "sp"), axis=0, tiled=True).reshape(cp_size, 2, BLK, 2, HD)
        holder = jnp.argsort(span_order)
        back = jnp.maximum(span_order[cp_index] - jnp.arange(reach + 1, dtype=jnp.int32), 0)
        chosen = pair[holder[back]]
        own, other = (chosen[0, k].reshape(BLK, 2 * HD) for k in (0, 1))
        picked, others = ([chosen[1:, k, :, part].reshape(reach * BLK, HD) for part in (0, 1)] for k in (0, 1))
    return attend(cp_size, meta, queries, own, other, *picked, *others)


def solution(mesh):
    in_specs = (P("cp", "sp"), P(("cp", "sp"), None), P(("cp", "sp"), None), P(), P())
    out_specs = P("cp", "sp")
    body = functools.partial(shards, mesh.shape["cp"], mesh.shape["sp"])
    return jax.shard_map(body, mesh=mesh, in_specs=in_specs, out_specs=out_specs, check_vma=False)
```

```python
import functools
import math

import jax
import jax.numpy as jnp
from jax import lax
from jax.experimental import pallas as pl
from jax.experimental.pallas import tpu as pltpu
from jax.sharding import PartitionSpec as P

HD = 128
SPAN = 256
BLK = 128
NEGATIVE = -1e30
HEAD = 2
SCALE2 = math.log2(math.e) / math.sqrt(HD)
LINES = ((3, 0), (1, 2))


def flip(array, axis, size, mask):
    return lax.ppermute(array, axis, [(i, i ^ mask) for i in range(size)])


def locate(apart):
    line = apart >> 2
    group = (line ^ (line >> 1)) & 1
    return group * 4 + (apart & 1) * 2 + ((apart >> 1) & 1), 1 - (line & 1)


def select_kernel(code_ref, *refs):
    sources, (keys_ref, values_ref) = refs[:-2], refs[-2:]
    for index in range(keys_ref.shape[0] // BLK):
        rows = slice(index * BLK, (index + 1) * BLK)
        code = code_ref[index, 0]
        for number, source in enumerate(sources):

            @pl.when((code >> 1) == number)
            def _():
                keys_ref[rows, :] = source[code & 1, :, 0:HD]
                values_ref[rows, :] = source[code & 1, :, HD:]


def extent(meta_ref, cp_size, half, reach):
    span = meta_ref[HEAD + meta_ref[0]]
    doc_at = HEAD + cp_size
    doc = meta_ref[doc_at + 2 * span]
    count = jnp.int32(0)
    for back in range(1, reach + 1):
        block = 2 * (span - back) + half
        held = (block >= 0) & (meta_ref[doc_at + jnp.maximum(block, 0)] == doc)
        count = count + jnp.where(held, 1, 0)
    return count, doc == meta_ref[doc_at + 2 * span + 1]


def stack_kernel(cp_size, reach, meta_ref, q_ref, out_ref, code_ref, sems):
    heads = out_ref.shape[1] // BLK
    copies = [
        pltpu.make_async_copy(
            q_ref.at[pl.ds(a * BLK, BLK), pl.ds(h * HD, HD)], out_ref.at[a, pl.ds(h * BLK, BLK), :], sems.at[a, h]
        )
        for a in range(2)
        for h in range(heads)
    ]
    for copy in copies:
        copy.start()
    cp = meta_ref[0, 0]
    order = [meta_ref[0, HEAD + index] for index in range(cp_size)]
    own_span = jnp.int32(0)
    for index in range(cp_size):
        own_span = jnp.where(cp == index, order[index], own_span)
    for back in range(1, reach + 1):
        span = jnp.maximum(own_span - back, 0)
        holder = jnp.int32(0)
        for index in range(cp_size):
            holder = jnp.where(order[index] == span, jnp.int32(index), holder)
        source, slot = locate(holder ^ cp)
        code_ref[back - 1 : back, :] = jnp.full((1, HD), source * 2 + slot, jnp.int32)
    for copy in copies:
        copy.wait()


def score(queries, keys):
    return lax.dot_general(queries, keys, (((1,), (1,)), ((), ())), preferred_element_type=jnp.float32)


def row_top(blocks):
    best = blocks[0]
    for block in blocks[1:]:
        best = jnp.maximum(best, block)
    return jnp.max(best, axis=1, keepdims=True)


def row_sum(blocks):
    added = blocks[0]
    for block in blocks[1:]:
        added = added + block
    return jnp.sum(added, axis=1, keepdims=True)


def split(scores):
    return [scores[:, c : c + BLK] for c in range(0, scores.shape[1], BLK)]


def with_ones(values):
    return jnp.concatenate([values, jnp.ones_like(values)], axis=1)


def cases(count, most, body):
    for n in range(most + 1):
        pl.when(count == n)(functools.partial(body, n))


def first_kernel(cp_size, chunk, meta_ref, q_ref, own_ref, other_ref, keys_ref, values_ref, max_ref, acc_ref, plan_ref):
    half = meta_ref[1]
    reach = keys_ref.shape[0] // BLK
    count, same = extent(meta_ref, cp_size, half, reach)
    beyond, same = extent(meta_ref, cp_size, 1 - half, reach)
    plan_ref[0:1, :] = jnp.full((1, HD), beyond, jnp.int32)
    plan_ref[1:2, :] = jnp.full((1, HD), jnp.where(same, 1, 0), jnp.int32)
    swap = half == 1
    mine, other = own_ref[...], other_ref[...]
    low, high = jnp.where(swap, other, mine), jnp.where(swap, mine, other)
    rows = lax.broadcasted_iota(jnp.int32, (BLK, BLK), 0)
    cols = lax.broadcasted_iota(jnp.int32, (BLK, BLK), 1)
    causal = jnp.where(cols <= rows, 0.0, NEGATIVE)
    causal = jnp.concatenate([causal] * chunk, axis=0)

    def attend(a, own, n):
        own_values = with_ones(own[:, HD:])
        for group in range(q_ref.shape[1] // (BLK * chunk)):
            at = slice(group * chunk * BLK, (group + 1) * chunk * BLK)
            queries = q_ref[a, at]
            blocks = split(score(queries, own[:, 0:HD]))
            blocks[-1] = blocks[-1] + causal
            if n:
                blocks = blocks + split(score(queries, keys_ref[0 : n * BLK, :]))
            top = row_top(blocks)
            weights = [jnp.exp2((block - top) * SCALE2).astype(jnp.bfloat16) for block in blocks]
            mid = own.shape[0] // BLK
            total = jnp.dot(
                jnp.concatenate(weights[:mid], axis=1), own_values, preferred_element_type=jnp.float32
            )
            if n:
                total = total + jnp.dot(
                    jnp.concatenate(weights[mid:], axis=1),
                    with_ones(values_ref[0 : n * BLK, :]),
                    preferred_element_type=jnp.float32,
                )
            max_ref[a, at] = jnp.broadcast_to(top, (chunk * BLK, HD))
            acc_ref[a, at] = total

    cases(count, reach, functools.partial(attend, 0, low))

    @pl.when(same)
    def _():
        cases(count, reach, functools.partial(attend, 1, jnp.concatenate([low, high], axis=0)))

    @pl.when(jnp.logical_not(same))
    def _():
        attend(1, high, 0)


def weigh_kernel(chunk, plan_ref, q_ref, keys_ref, max_ref, acc_ref, weights_ref, rest_ref):
    reach = keys_ref.shape[0] // BLK
    count, same = plan_ref[0, 0], plan_ref[1, 0] == 1

    def weigh(a, n):
        for group in range(q_ref.shape[1] // (BLK * chunk)):
            at = slice(group * chunk * BLK, (group + 1) * chunk * BLK)
            old, total = acc_ref[a, at, 0:HD], acc_ref[a, at, HD:]
            if n:
                blocks = split(score(q_ref[a, at], keys_ref[0 : n * BLK, :]))
                old_top = max_ref[a, at]
                top = jnp.maximum(row_top(blocks), old_top)
                fade = jnp.exp2((old_top - top) * SCALE2)
                blocks = [jnp.exp2((block - top) * SCALE2) for block in blocks]
                share = 1.0 / (total * fade + row_sum(blocks))
                for index, block in enumerate(blocks):
                    weights_ref[a, at, index * BLK : (index + 1) * BLK] = (block * share).astype(jnp.bfloat16)
                rest_ref[a, at] = old * (fade * share)
            else:
                rest_ref[a, at] = old / total
            empty = reach - n
            if empty:
                weights_ref[a, at, n * BLK :] = jnp.zeros((chunk * BLK, empty * BLK), jnp.bfloat16)

    for a in range(2):
        cases(count if a == 0 else jnp.where(same, count, 0), reach, functools.partial(weigh, a))


def finish_kernel(chunk, plan_ref, weights_ref, rest_ref, values_ref, out_ref, done, sems):
    reach = values_ref.shape[0] // BLK
    groups = rest_ref.shape[1] // (BLK * chunk)
    places = [(a, group) for a in range(2) for group in range(groups)]
    copies = [
        pltpu.make_async_copy(
            done.at[a, group],
            out_ref.at[pl.ds(a * BLK, BLK), pl.ds(group * chunk * HD, chunk * HD)],
            sems.at[a, group],
        )
        for a, group in places
    ]

    def finish(pairs):
        depth = min(2 * pairs, reach) * BLK
        for (a, group), copy in zip(places, copies):
            at = slice(group * chunk * BLK, (group + 1) * chunk * BLK)
            result = rest_ref[a, at]
            if depth:
                result = result + jnp.dot(
                    weights_ref[a, at, 0:depth], values_ref[0:depth, :], preferred_element_type=jnp.float32
                )
            result = result.astype(done.dtype)
            for h in range(chunk):
                done[a, group, :, h * HD : (h + 1) * HD] = result[h * BLK : (h + 1) * BLK]
            copy.start()
        for copy in copies:
            copy.wait()

    cases((plan_ref[0, 0] + 1) // 2, (reach + 1) // 2, finish)


VMEM = pl.BlockSpec(memory_space=pltpu.VMEM)
SMEM = pl.BlockSpec(memory_space=pltpu.SMEM)
ANY = pl.BlockSpec(memory_space=pl.ANY)


def local_call(kernel, name, outs, in_specs, grant, flops, **extra):
    return pl.pallas_call(
        kernel,
        out_shape=outs,
        in_specs=in_specs,
        compiler_params=pltpu.CompilerParams(vmem_limit_bytes=grant * 1024 * 1024),
        cost_estimate=pl.CostEstimate(flops=flops, bytes_accessed=1 << 20, transcendentals=0),
        name=name,
        **{"out_specs": [VMEM] * len(outs), **extra},
    )


def stack_queries(cp_size, reach, meta, queries):
    heads = queries.shape[1] // HD
    outs = [
        jax.ShapeDtypeStruct((2, heads * BLK, HD), queries.dtype),
        jax.ShapeDtypeStruct(((reach + 7) // 8 * 8, HD), jnp.int32),
    ]
    scratch = [pltpu.SemaphoreType.DMA((2, heads))]
    kernel = functools.partial(stack_kernel, cp_size, reach)
    return local_call(kernel, "stack_queries", outs, [VMEM, ANY], 4, 1 << 20, scratch_shapes=scratch)(meta[None], queries)


def attend(cp_size, meta, queries, own, other, keys, values, other_keys, other_values):
    reach, rows = keys.shape[0] // BLK, queries.shape[1]
    chunk = min(rows // BLK, 4)
    groups = rows // (BLK * chunk)
    state = lambda width, dtype=jnp.float32: jax.ShapeDtypeStruct((2, rows, width), dtype)
    kernel = functools.partial(first_kernel, cp_size, chunk)
    outs = [state(HD), state(2 * HD), jax.ShapeDtypeStruct((8, HD), jnp.int32)]
    ins = [SMEM] + [VMEM] * 5
    first = local_call(kernel, "attend_first", outs, ins, 12, 1 << 31)
    top, acc, plan = first(meta, queries, own, other, keys, values)
    kernel = functools.partial(weigh_kernel, chunk)
    outs, ins = [state(reach * BLK, jnp.bfloat16), state(HD)], [VMEM] * 5
    weights, rest = local_call(kernel, "attend_weigh", outs, ins, 12, 1 << 30)(plan, queries, other_keys, top, acc)
    outs = [jax.ShapeDtypeStruct((2 * BLK, rows // BLK * HD), queries.dtype)]
    scratch = [
        pltpu.VMEM((2, groups, BLK, chunk * HD), queries.dtype),
        pltpu.SemaphoreType.DMA((2, groups)),
    ]
    kernel = functools.partial(finish_kernel, chunk)
    finish = local_call(
        kernel, "attend_finish", outs, [VMEM] * 4, 8, 1 << 29, out_specs=[ANY], scratch_shapes=scratch
    )
    return finish(plan, weights, rest, other_values)[0]


def shards(cp_size, sp_size, queries, keys, values, doc_ids, span_order):
    reach = doc_ids.shape[0] // 8
    staged = cp_size == 16 and sp_size == 2
    cp_index = lax.axis_index("cp").astype(jnp.int32)
    half = lax.axis_index("sp").astype(jnp.int32) if staged else jnp.int32(0)
    meta = jnp.concatenate([jnp.stack([cp_index, half]), span_order, doc_ids])
    own = lax.pad(keys, jnp.bfloat16(0), ((0, 0, 0), (0, HD, 0)))
    own = own + lax.pad(values, jnp.bfloat16(0), ((0, 0, 0), (HD, 0, 0)))
    queries, codes = stack_queries(cp_size, reach, meta, queries)
    if staged:
        by_x = lambda array: flip(array, "cp", cp_size, 2)
        by_y = lambda array: flip(array, "sp", sp_size, 1)
        by_core = lambda array: flip(array, "cp", cp_size, 1)
        far = {j: flip(own, "cp", cp_size, 4 * j) for j in (3, 2, 1)}
        far[1], far[2], queries, meta = lax.optimization_barrier((far[1], far[2], queries, meta))
        far[0] = own
        sources = []
        for group in LINES:
            line = jnp.stack([far[j] for j in group])
            side = by_x(line)
            sources += [line, side, by_core(line), by_core(side)]
        sources[5], own_late = lax.optimization_barrier((sources[5], own))
        other = by_y(own_late)
        part = jax.ShapeDtypeStruct((reach * BLK, HD), jnp.bfloat16)
        picked = local_call(
            select_kernel, "select", [part] * 2, [VMEM] * (1 + len(sources)), 4, 1 << 20
        )(codes, *sources)
        others = [by_y(array) for array in picked]
    else:
        pair = lax.all_gather(own, ("cp", "sp"), axis=0, tiled=True).reshape(cp_size, 2, BLK, 2, HD)
        holder = jnp.argsort(span_order)
        back = jnp.maximum(span_order[cp_index] - jnp.arange(reach + 1, dtype=jnp.int32), 0)
        chosen = pair[holder[back]]
        own, other = (chosen[0, k].reshape(BLK, 2 * HD) for k in (0, 1))
        picked, others = ([chosen[1:, k, :, part].reshape(reach * BLK, HD) for part in (0, 1)] for k in (0, 1))
    return attend(cp_size, meta, queries, own, other, *picked, *others)


def solution(mesh):
    in_specs = (P("cp", "sp"), P(("cp", "sp"), None), P(("cp", "sp"), None), P(), P())
    out_specs = P("cp", "sp")
    body = functools.partial(shards, mesh.shape["cp"], mesh.shape["sp"])
    return jax.shard_map(body, mesh=mesh, in_specs=in_specs, out_specs=out_specs, check_vma=False)
```
